512 devices in a mesh: row: 16 (over x, z_lo, core), col: 4 (over z_hi), depth: 8 (over y).
Axes of the slice: x: 4, y: 8, z: 8 (z_hi: 4, z_lo: 2; z = z_hi * 2 + z_lo), core: 2. Of those that a mesh axis runs over, the one named last changes fastest.
Arguments:
- normed: bfloat16 [4096, 3072], P(('depth', 'row'), 'col'), may hold values from -6 to 6
- up_weight: bfloat16 [3072, 12288], P('col', 'row'), may hold values from -0.109375 to 0.109375
- down_weight: bfloat16 [12288, 3072], P('row', 'col'), may hold values from -0.0546875 to 0.0546875
- out_grad: bfloat16 [4096, 3072], P(('depth', 'row'), 'col'), may hold values from -6 to 6
Outputs:
- branch_out: bfloat16 [4096, 3072], P(('depth', 'row'), 'col')
- normed_grad: bfloat16 [4096, 3072], P(('depth', 'row'), 'col')
- up_grad: float32 [3072, 12288], P(('col', 'depth'), 'row')
- down_grad: float32 [12288, 3072], P(('row', 'depth'), 'col')
The draws below stay inside these ranges and needn't reach their ends.
All inputs are finite; a program needn't handle non-finite values.
Results may differ from the reference program's by a relative error of at most 0.029.
Values may be sent and summed in bfloat16 or wider, within the bound.
A program may use at most 64 MiB of HBM per device.

```python
import math
import jax
import jax.numpy as jnp
from jax import lax

D = 3072
F = 12288
TOKENS = 4096
N_ROW = 16
N_COL = 4
N_DEPTH = 8


def steps_of(stream_key, extent, pieces, least, top_value):
    def one(dim, blocks):
        heights = jax.random.uniform(jax.random.fold_in(jax.random.fold_in(stream_key, 6), dim), (blocks,), jnp.float32, least / len(pieces), top_value / len(pieces))
        return jnp.repeat(jnp.exp(heights), extent[dim] // blocks).reshape((-1,) + (1,) * (len(extent) - dim - 1))

    gain = one(*pieces[0])
    for cut in pieces[1:]:
        gain = gain * one(*cut)
    return gain


def centred(stream_key, extent, deviation, bound, cuts=(), kind=jnp.bfloat16):
    array = deviation * jax.random.normal(stream_key, extent, jnp.float32)
    if cuts:
        array = array * steps_of(stream_key, extent, cuts, -0.22, 0.18)
    return jnp.clip(array, -bound, bound).astype(kind)


def setup_inputs(seed: int = 0) -> dict:
    arg_keys = jax.random.split(jax.random.key(seed), 5)
    normed = centred(arg_keys[0], (TOKENS, D), 1.0, 6.0, ((0, 128), (1, 4)))
    up_weight = centred(arg_keys[1], (D, F), D ** -0.5, 0.109375, ((0, 4), (1, 16)))
    down_weight = centred(arg_keys[2], (F, D), F ** -0.5, 0.0546875, ((0, 16), (1, 4)))
    out_grad = centred(arg_keys[3], (TOKENS, D), 1.0, 6.0, ((0, 128), (1, 4)))
    return dict(normed=normed, up_weight=up_weight, down_weight=down_weight, out_grad=out_grad)


def rounded(value):
    return lax.optimization_barrier(value.astype(jnp.bfloat16)).astype(jnp.float32)

def gelu_parts(value):
    coeff = math.sqrt(2.0 / math.pi)
    inner = coeff * (value + 0.044715 * value * value * value)
    tangent = jnp.tanh(inner)
    activated = 0.5 * value * (1.0 + tangent)
    slope = 0.5 * (1.0 + tangent) + 0.5 * value * (1.0 - tangent * tangent) * coeff * (1.0 + 3.0 * 0.044715 * value * value)
    return (activated, slope)

def reference(normed, up_weight, down_weight, out_grad):
    col_width = D // N_COL
    row_width = F // N_ROW
    layer_rows = TOKENS // N_DEPTH
    pre_act = jnp.zeros((TOKENS, F), jnp.float32)
    back_act = jnp.zeros((TOKENS, F), jnp.float32)
    for block in range(N_COL):
        lower = block * col_width
        upper = lower + col_width
        pre_act = pre_act + rounded(jnp.dot(normed[:, lower:upper], up_weight[lower:upper, :], preferred_element_type=jnp.float32))
        back_act = back_act + rounded(jnp.dot(out_grad[:, lower:upper], down_weight[:, lower:upper].T, preferred_element_type=jnp.float32))
    active_full, slope = gelu_parts(pre_act)
    activated = active_full.astype(jnp.bfloat16)
    pre_grad = (back_act * slope).astype(jnp.bfloat16)
    branch_out = jnp.zeros((TOKENS, D), jnp.float32)
    normed_grad = jnp.zeros((TOKENS, D), jnp.float32)
    for block in range(N_ROW):
        lower = block * row_width
        upper = lower + row_width
        branch_out = branch_out + rounded(jnp.dot(activated[:, lower:upper], down_weight[lower:upper, :], preferred_element_type=jnp.float32))
        normed_grad = normed_grad + rounded(jnp.dot(pre_grad[:, lower:upper], up_weight[:, lower:upper].T, preferred_element_type=jnp.float32))
    up_grad = jnp.zeros((D, F), jnp.float32)
    down_grad = jnp.zeros((F, D), jnp.float32)
    for layer in range(N_DEPTH):
        lower = layer * layer_rows
        upper = lower + layer_rows
        up_grad = up_grad + rounded(jnp.dot(normed[lower:upper].T, pre_grad[lower:upper], preferred_element_type=jnp.float32))
        down_grad = down_grad + rounded(jnp.dot(activated[lower:upper].T, out_grad[lower:upper], preferred_element_type=jnp.float32))
    factor = 1.0 / math.sqrt(TOKENS)
    return (branch_out.astype(jnp.bfloat16), normed_grad.astype(jnp.bfloat16), up_grad * factor, down_grad * factor)
```

```python
import functools
import math

import jax
import jax.numpy as jnp
from jax import lax
from jax.experimental import pallas as pl
from jax.experimental.pallas import tpu as pltpu
from jax.sharding import PartitionSpec as P

MESH = pl.DeviceIdType.MESH
BF16, F32 = jnp.bfloat16, jnp.float32
TOKEN_PARTS = 2
HIDDEN_PARTS = 6
ROLLED = True


def dot(left, right):
    return jnp.dot(left, right, preferred_element_type=F32)


def contract_last(left, right):
    return lax.dot_general(left, right, (((1,), (1,)), ((), ())), preferred_element_type=F32)


def contract_first(left, right):
    return lax.dot_general(left, right, (((0,), (0,)), ((), ())), preferred_element_type=F32)


def gelu_parts(value):
    coeff = math.sqrt(2.0 / math.pi)
    square = value * value
    tangent = jnp.tanh(coeff * (value + 0.044715 * square * value))
    half = 0.5 * (1.0 + tangent)
    slope = half + 0.5 * value * (1.0 - tangent * tangent) * coeff * (1.0 + 3.0 * 0.044715 * square)
    return value * half, slope


def add(first, second):
    return (first.astype(F32) + second.astype(F32)).astype(BF16)


def when(condition, action):
    if isinstance(condition, bool):
        if condition:
            action()
    else:
        pl.when(condition)(action)


def both(low, value, high):
    if isinstance(value, int):
        return low <= value < high
    return jnp.logical_and(value >= low, value < high)


def kernel(
    shape, factor,
    normed, up_weight, down_weight, out_grad,
    branch_out, normed_grad, up_grad, down_grad,
    tokens, tokens_t, perm, up_perm, down_perm,
    part, half_in, full_in, acts,
    grads, grads_in, rows, rows_in, ring, ring_half, ring_full, last, last_send, last_in,
    a_send, a_recv, z_send, z_recv, y_send, y_recv, r_send, r_recv,
):
    tn, hn, m, q, w, rt, n_depth = shape
    units = tn * hn
    slab = w // n_depth
    row, col, depth = lax.axis_index("row"), lax.axis_index("col"), lax.axis_index("depth")
    x, zl, core = row // 4, lax.rem(row // 2, 2), lax.rem(row, 2)

    def at_row(x_, zl_, core_):
        return x_ * 4 + zl_ * 2 + core_

    def ring_step(index, by, size):
        return lax.rem(index + by + size, size)

    right, left, opposite = (ring_step(col, by, 4) for by in (1, -1, 2))
    x_right, x_left, x_opposite = (ring_step(x, by, 4) for by in (1, -1, 2))
    to_right, to_left = {"col": right}, {"col": left}
    to_xr, to_xl = {"row": at_row(x_right, zl, core)}, {"row": at_row(x_left, zl, core)}
    to_zp, to_sib = {"row": at_row(x, 1 - zl, core)}, {"row": at_row(x, zl, 1 - core)}
    to_yr = {"depth": ring_step(depth, 1, n_depth)}
    to_yl = {"depth": ring_step(depth, -1, n_depth)}

    def copy(src, dst, send, recv, to):
        return pltpu.make_async_remote_copy(
            src_ref=src, dst_ref=dst, send_sem=send, recv_sem=recv, device_id=to, device_id_type=MESH
        )

    def got(dst, recv):
        copy(dst, dst, recv, recv, to_sib).wait_recv()

    def sent(src, send):
        copy(src, src, send, send, to_sib).wait_send()

    barrier = pltpu.get_barrier_semaphore()
    for to in (to_right, to_left, to_xr, to_xl, to_zp, to_sib, to_yr, to_yl):
        pl.semaphore_signal(barrier, inc=1, device_id=to, device_id_type=MESH)

    for t in range(tn):
        tokens[t, 0, row] = normed[t * rt : (t + 1) * rt, :]
        tokens[t, 1, row] = out_grad[t * rt : (t + 1) * rt, :]
    pl.semaphore_wait(barrier, 8)

    other = 1 - zl
    origin = [
        at_row(x, zl, core), at_row(x, other, core),
        at_row(x_left, zl, core), at_row(x_right, zl, core),
        at_row(x_left, other, core), at_row(x_right, other, core),
        at_row(x_opposite, zl, core), at_row(x_opposite, other, core),
    ]
    sib_origin = [at_row(x_, z_, 1 - core) for x_, z_ in (
        (x, zl), (x, other), (x_left, zl), (x_right, zl), (x_left, other), (x_right, other),
        (x_opposite, zl), (x_opposite, other))]

    def a_copy(t, src, to, send, recv):
        return copy(src, src, a_send.at[t, send], a_recv.at[t, recv], to)

    def piece(t, index):
        return tokens.at[t, :, origin[index]]

    def half(t, index, array):
        return tokens.at[t, array, origin[index]]

    def gather_1(t):
        a_copy(t, piece(t, 0), to_xr, 1, 1).start()
        a_copy(t, piece(t, 0), to_xl, 2, 2).start()
        a_copy(t, piece(t, 0), to_zp, 0, 0).start()
        a_copy(t, piece(t, 0), to_sib, 9, 9).start()

    def gather_2(t):
        got(piece(t, 1), a_recv.at[t, 0])
        a_copy(t, piece(t, 1), to_xr, 3, 3).start()
        a_copy(t, piece(t, 1), to_xl, 4, 4).start()
        got(piece(t, 2), a_recv.at[t, 1])
        a_copy(t, half(t, 2, 0), to_xr, 5, 5).start()
        got(piece(t, 3), a_recv.at[t, 2])
        a_copy(t, half(t, 3, 1), to_xl, 6, 6).start()
        for index in (1, 2, 3):
            a_copy(t, piece(t, index), to_sib, 9 + index, 9 + index).start()

    def gather_3(t):
        got(piece(t, 4), a_recv.at[t, 3])
        a_copy(t, half(t, 4, 0), to_xr, 7, 7).start()
        got(piece(t, 5), a_recv.at[t, 4])
        a_copy(t, half(t, 5, 1), to_xl, 8, 8).start()
        for index in (4, 5):
            a_copy(t, piece(t, index), to_sib, 9 + index, 9 + index).start()

    def gather_4(t):
        for index in (6, 7):
            got(half(t, index, 0), a_recv.at[t, 2 * index - 7])
            got(half(t, index, 1), a_recv.at[t, 2 * index - 6])
            a_copy(t, piece(t, index), to_sib, 9 + index, 9 + index).start()

    def gather_5(t):
        for index in range(8):
            got(tokens.at[t, :, sib_origin[index]], a_recv.at[t, 9 + index])
        tokens_t[t] = tokens[t, 0].reshape(m, -1).T
        for send, index in ((0, 0), (1, 0), (2, 0), (3, 1), (4, 1)):
            sent(piece(t, index), a_send.at[t, send])
        for send, index, array in ((5, 2, 0), (6, 3, 1), (7, 4, 0), (8, 5, 1)):
            sent(half(t, index, array), a_send.at[t, send])
        for index in range(8):
            sent(piece(t, index), a_send.at[t, 9 + index])

    gather_1(0)
    extent = up_weight.shape[1]
    for h in range(hn):
        inner = lax.broadcasted_iota(jnp.int32, (extent, w), 1)
        wanted = (inner // slab) * (extent // n_depth) + h * slab + lax.rem(inner, slab)
        perm[h] = jnp.where(lax.broadcasted_iota(jnp.int32, (extent, w), 0) == wanted, 1.0, 0.0).astype(BF16)
        up_perm[h] = dot(up_weight[...], perm[h]).astype(BF16)
        for d in range(n_depth):
            base = d * (extent // n_depth) + h * slab
            down_perm[h, d * slab : (d + 1) * slab, :] = down_weight[base : base + slab, :]
    gather_2(0)
    for t in range(1, tn):
        gather_1(t)
    gather_3(0)
    for t in range(1, tn):
        gather_2(t)
    gather_4(0)
    for t in range(1, tn):
        gather_3(t)
    gather_5(0)

    def split(unit):
        return unit // hn, unit % hn

    def stage_f(u):
        t, h = split(u)
        up = dot(tokens[t, 0].reshape(m, -1), up_perm[h]).astype(BF16)
        part[u, :, 0] = up.reshape(4, q, w)
        back = contract_last(tokens[t, 1].reshape(m, -1), down_perm[h]).astype(BF16)
        part[u, :, 1] = back.reshape(4, q, w)
        copy(part.at[u, opposite, 0], half_in.at[u, 0], z_send.at[u, 0], z_recv.at[u, 0], to_right).start()
        copy(part.at[u, opposite, 1], half_in.at[u, 1], z_send.at[u, 1], z_recv.at[u, 1], to_left).start()

    def stage_r1(u):
        got(half_in.at[u, 0], z_recv.at[u, 0])
        part[u, right, 0] = add(part[u, right, 0], half_in[u, 0])
        copy(part.at[u, right], full_in.at[u, 0], z_send.at[u, 2], z_recv.at[u, 2], to_right).start()
        got(half_in.at[u, 1], z_recv.at[u, 1])
        part[u, left, 1] = add(part[u, left, 1], half_in[u, 1])
        copy(part.at[u, left], full_in.at[u, 1], z_send.at[u, 3], z_recv.at[u, 3], to_left).start()

    def stage_r2(u):
        got(full_in.at[u, 0], z_recv.at[u, 2])
        got(full_in.at[u, 1], z_recv.at[u, 3])
        total = part[u, col].astype(F32) + full_in[u, 0].astype(F32) + full_in[u, 1].astype(F32)
        active, slope = gelu_parts(total[0])
        acts[u, 0, col] = active.astype(BF16)
        acts[u, 1, col] = (total[1] * slope).astype(BF16)
        mine = acts.at[u, :, col]
        copy(mine, mine, z_send.at[u, 4], z_recv.at[u, 4], to_right).start()
        copy(mine, mine, z_send.at[u, 5], z_recv.at[u, 5], to_left).start()
        sent(part.at[u, opposite, 0], z_send.at[u, 0])
        sent(part.at[u, opposite, 1], z_send.at[u, 1])

    def stage_a1(u):
        got(acts.at[u, :, left], z_recv.at[u, 4])
        copy(acts.at[u, 0, left], acts.at[u, 0, left], z_send.at[u, 6], z_recv.at[u, 6], to_right).start()
        got(acts.at[u, :, right], z_recv.at[u, 5])
        copy(acts.at[u, 1, right], acts.at[u, 1, right], z_send.at[u, 7], z_recv.at[u, 7], to_left).start()
        sent(part.at[u, right], z_send.at[u, 2])
        sent(part.at[u, left], z_send.at[u, 3])

    def y_copies(h, step):
        if step == 0:
            far = ring_step(depth, n_depth // 2, n_depth)
            pairs = (
                (grads.at[h, far, 0], grads_in.at[h, 0, 0, 0]),
                (grads.at[h, far, 1], grads_in.at[h, 0, 1, 1]),
            )
        else:
            away = n_depth // 2 - step
            pairs = (
                (grads.at[h, ring_step(depth, away, n_depth)], grads_in.at[h, step, 0]),
                (grads.at[h, ring_step(depth, -away, n_depth)], grads_in.at[h, step, 1]),
            )
        return tuple(
            copy(src, dst, y_send.at[h, step, way], y_recv.at[h, step, way], to)
            for way, ((src, dst), to) in enumerate(zip(pairs, (to_yr, to_yl)))
        )

    y_steps = n_depth // 2

    def stage_y(h, step):
        before = y_copies(h, step - 1)
        if step == y_steps:
            before[0].wait_recv()
            before[1].wait_recv()
            total = (
                grads[h, depth].astype(F32) + grads_in[h, step - 1, 0].astype(F32) + grads_in[h, step - 1, 1].astype(F32)
            ) * factor
            down_grad[pl.ds(pl.multiple_of(h * slab, slab), slab), :] = total[1]
            block = jnp.concatenate([total[0, :, j * w : (j + 1) * w] for j in range(hn)], axis=0)
            high = block.astype(BF16)
            low = (block - high.astype(F32)).astype(BF16)
            spread = contract_last(high, perm[h]) + contract_last(low, perm[h])
            up_grad[...] = up_grad[...] + spread
        else:
            now = y_copies(h, step)
            for way, sign in ((0, 1), (1, -1)):
                before[way].wait_recv()
                owner = ring_step(depth, sign * (y_steps - step), n_depth)
                if step == 1:
                    grads[h, owner, way] = add(grads[h, owner, way], grads_in[h, 0, way, way])
                else:
                    grads[h, owner] = add(grads[h, owner], grads_in[h, step - 1, way])
                now[way].start()
        before[0].wait_send()
        before[1].wait_send()

    def row_copies(t, step):
        if step == 0:
            return (copy(rows.at[t, :, :, 1 - core], rows_in.at[t], r_send.at[t, 0], r_recv.at[t, 0], to_sib),)
        if step == 1:
            return (
                copy(ring.at[t, x_opposite, 0], ring_half.at[t, 0], r_send.at[t, 1], r_recv.at[t, 1], to_xr),
                copy(ring.at[t, x_opposite, 1], ring_half.at[t, 1], r_send.at[t, 2], r_recv.at[t, 2], to_xl),
            )
        if step == 2:
            return (
                copy(ring.at[t, x_right], ring_full.at[t, 0], r_send.at[t, 3], r_recv.at[t, 3], to_xr),
                copy(ring.at[t, x_left], ring_full.at[t, 1], r_send.at[t, 4], r_recv.at[t, 4], to_xl),
            )
        return (copy(last_send.at[t], last_in.at[t], r_send.at[t, 5], r_recv.at[t, 5], to_zp),)

    def stage_row(t, step):
        before = row_copies(t, step - 1)
        now = row_copies(t, step) if step < 4 else ()
        if step == 1:
            before[0].wait_recv()
            for xs in range(4):
                for array in range(2):
                    ring[t, xs, array] = add(rows[t, array, 2 * xs : 2 * xs + 2, core], rows_in[t, array, 2 * xs : 2 * xs + 2])
        elif step == 2:
            before[0].wait_recv()
            ring[t, x_right, 0] = add(ring[t, x_right, 0], ring_half[t, 0])
            before[1].wait_recv()
            ring[t, x_left, 1] = add(ring[t, x_left, 1], ring_half[t, 1])
        elif step == 3:
            before[0].wait_recv()
            before[1].wait_recv()
            last[t] = ring[t, x].astype(F32) + ring_full[t, 0].astype(F32) + ring_full[t, 1].astype(F32)
            last_send[t] = last[t, :, 1 - zl].astype(BF16)
        else:
            before[0].wait_recv()
            total = (last[t, :, zl] + last_in[t].astype(F32)).astype(BF16)
            here = pl.ds(t * rt if isinstance(t, int) else pl.multiple_of(t * rt, rt), rt)
            branch_out[here, :] = total[0]
            normed_grad[here, :] = total[1]
        for one in now:
            one.start()
        for one in before:
            one.wait_send()

    def stage_b(u):
        t, h = split(u)
        got(acts.at[u, 0, opposite], z_recv.at[u, 6])
        got(acts.at[u, 1, opposite], z_recv.at[u, 7])

        def weight_grads():
            up = sum(dot(tokens_t[s], acts[s * hn + h, 1].reshape(m, w)) for s in range(tn)).astype(BF16)
            down = sum(
                contract_first(acts[s * hn + h, 0].reshape(m, w), tokens[s, 1].reshape(m, -1)) for s in range(tn)
            ).astype(BF16)
            for d in range(n_depth):
                for j in range(hn):
                    base = d * slab * hn + j * slab
                    grads[h, d, 0, :, j * w : (j + 1) * w] = up[base : base + slab, :]
                grads[h, d, 1] = down[d * slab : (d + 1) * slab, :]
            for one in y_copies(h, 0):
                one.start()

        def token_sums():
            active = jnp.concatenate([acts[t * hn + i, 0].reshape(m, w) for i in range(hn)], axis=1)
            out = dot(active, down_perm[...].reshape(hn * w, -1)).astype(BF16)
            rows[t, 0] = out.reshape(8, 2, rt, -1)
            cotangent = jnp.concatenate([acts[t * hn + i, 1].reshape(m, w) for i in range(hn)], axis=1)
            weight = jnp.concatenate([up_perm[i] for i in range(hn)], axis=1)
            back = contract_last(cotangent, weight).astype(BF16)
            rows[t, 1] = back.reshape(8, 2, rt, -1)
            for one in row_copies(t, 0):
                one.start()

        when(h == hn - 1, token_sums)
        when(t == tn - 1, weight_grads)
        sent(acts.at[u, :, col], z_send.at[u, 4])
        sent(acts.at[u, :, col], z_send.at[u, 5])
        sent(acts.at[u, 0, left], z_send.at[u, 6])
        sent(acts.at[u, 1, right], z_send.at[u, 7])

    up_grad[...] = jnp.zeros_like(up_grad)
    first_y = (tn - 1) * hn + 4

    def turn(k):
        for t in range(1, tn):
            when(k == (t - 1) * hn + 1, functools.partial(gather_4, t))
            when(k == t * hn, functools.partial(gather_5, t))
        when(both(0, k, units), lambda: stage_f(k))
        when(both(1, k, units + 1), lambda: stage_r1(k - 1))
        when(both(2, k, units + 2), lambda: stage_r2(k - 2))
        when(both(3, k, units + 3), lambda: stage_a1(k - 3))
        for step in range(1, 5):
            for t in range(tn):
                when(k == t * hn + hn + 3 + step, functools.partial(stage_row, t, step))
        for step in range(1, y_steps + 1):
            when(
                both(first_y + step, k, first_y + step + hn),
                lambda step=step: stage_y(k - first_y - step, step),
            )
        when(both(4, k, units + 4), lambda: stage_b(k - 4))

    turns = units + 4 + max(4, y_steps)
    if ROLLED:
        pl.loop(0, turns)(turn)
    else:
        for k in range(turns):
            turn(k)


def solution(mesh):
    n_row, n_col, n_depth = (mesh.shape[name] for name in ("row", "col", "depth"))
    tn, hn = TOKEN_PARTS, HIDDEN_PARTS

    def per_device(normed, up_weight, down_weight, out_grad):
        block, width = normed.shape
        hidden = up_weight.shape[1]
        rt, w = block // tn, hidden // hn
        m = rt * n_row
        q = m // n_col
        slab = w // n_depth
        units = tn * hn
        factor = 1.0 / math.sqrt(block * n_row * n_depth)
        dma = pltpu.SemaphoreType.DMA
        vmem = pltpu.VMEM
        whole = pl.BlockSpec(memory_space=pltpu.VMEM)
        return pl.pallas_call(
            functools.partial(kernel, (tn, hn, m, q, w, rt, n_depth), factor),
            out_shape=(
                jax.ShapeDtypeStruct((block, width), BF16),
                jax.ShapeDtypeStruct((block, width), BF16),
                jax.ShapeDtypeStruct((width // n_depth, hidden), F32),
                jax.ShapeDtypeStruct((hidden // n_depth, width), F32),
            ),
            in_specs=[whole] * 4,
            out_specs=[whole] * 4,
            scratch_shapes=[
                vmem((tn, 2, n_row, rt, width), BF16),
                vmem((tn, width, m), BF16),
                vmem((hn, hidden, w), BF16),
                vmem((hn, width, w), BF16),
                vmem((hn, w, width), BF16),
                vmem((units, n_col, 2, q, w), BF16),
                vmem((units, 2, q, w), BF16),
                vmem((units, 2, 2, q, w), BF16),
                vmem((units, 2, n_col, q, w), BF16),
                vmem((hn, n_depth, 2, slab, width), BF16),
                vmem((hn, n_depth // 2, 2, 2, slab, width), BF16),
                vmem((tn, 2, n_row // 2, 2, rt, width), BF16),
                vmem((tn, 2, n_row // 2, rt, width), BF16),
                vmem((tn, 4, 2, 2, rt, width), BF16),
                vmem((tn, 2, 2, rt, width), BF16),
                vmem((tn, 2, 2, 2, rt, width), BF16),
                vmem((tn, 2, 2, rt, width), F32),
                vmem((tn, 2, rt, width), BF16),
                vmem((tn, 2, rt, width), BF16),
                dma((tn, 17)), dma((tn, 17)),
                dma((units, 8)), dma((units, 8)),
                dma((hn, n_depth // 2, 2)), dma((hn, n_depth // 2, 2)),
                dma((tn, 6)), dma((tn, 6)),
            ],
            compiler_params=pltpu.CompilerParams(
                collective_id=0, has_side_effects=True, vmem_limit_bytes=56 * 1024 * 1024
            ),
            cost_estimate=pl.CostEstimate(flops=4_000_000_000, bytes_accessed=4_000_000, transcendentals=400_000),
        )(normed, up_weight, down_weight, out_grad)

    return jax.shard_map(
        per_device,
        mesh=mesh,
        in_specs=(P(("depth", "row"), "col"), P("col", "row"), P("row", "col"), P(("depth", "row"), "col")),
        out_specs=(
            P(("depth", "row"), "col"),
            P(("depth", "row"), "col"),
            P(("col", "depth"), "row"),
            P(("row", "depth"), "col"),
        ),
        check_vma=False,
    )
```

```python
import functools
import math

import jax
import jax.numpy as jnp
from jax import lax
from jax.experimental import pallas as pl
from jax.experimental.pallas import tpu as pltpu
from jax.sharding import PartitionSpec as P

MESH = pl.DeviceIdType.MESH
BF16, F32 = jnp.bfloat16, jnp.float32
NX, NZ, NC = 4, 8, 4


def dot(left, right):
    return jnp.dot(left, right, preferred_element_type=F32)


def contract_last(left, right):
    return lax.dot_general(left, right, (((1,), (1,)), ((), ())), preferred_element_type=F32)


def contract_first(left, right):
    return lax.dot_general(left, right, (((0,), (0,)), ((), ())), preferred_element_type=F32)


def gelu_parts(value):
    coeff = math.sqrt(2.0 / math.pi)
    square = value * value
    tangent = jnp.tanh(coeff * (value + 0.044715 * square * value))
    half = 0.5 * (1.0 + tangent)
    slope = half + 0.5 * value * (1.0 - tangent * tangent) * coeff * (1.0 + 3.0 * 0.044715 * square)
    return value * half, slope


def add(first, second):
    return (first.astype(F32) + second.astype(F32)).astype(BF16)


def wrap(index, by, size):
    return lax.rem(index + by + size, size)


def kernel(
    shape, factor,
    normed, up_weight, down_weight, out_grad,
    branch_out, normed_grad, up_grad, down_grad,
    tokens, perm, w_own, weights, up_share,
    act, pre_grad, grads, grads_sib, grads_in, grads_own, grads_back,
    out, out_half, out_full, ring, ring_in,
    t_send, t_recv, tx_send, tx_recv, a_send, a_recv, w_send, w_recv, s_send, s_recv,
    g_send, g_recv, y_send, y_recv, b_send, b_recv, x_send, x_recv, z_send, z_recv,
):
    block, m, share, slab, ny = shape
    width = normed.shape[1]
    hidden = up_weight.shape[1]
    lanes = width // 2
    row, k, depth = lax.axis_index("row"), lax.axis_index("col"), lax.axis_index("depth")
    x, zl, core = row // 4, lax.rem(row // 2, 2), lax.rem(row, 2)
    z = 2 * k + zl
    holder, half_of = k // 2, lax.rem(k, 2)

    def at(x_, z_, core_):
        return {"row": x_ * 4 + lax.rem(z_, 2) * 2 + core_, "col": z_ // 2}

    def peer(k_, core_):
        return {"row": x * 4 + zl * 2 + core_, "col": k_}

    x_right, x_left, x_far = wrap(x, 1, NX), wrap(x, -1, NX), wrap(x, 2, NX)
    to_x = (at(x_right, z, core), at(x_left, z, core))
    to_z = (at(x, wrap(z, 1, NZ), core), at(x, wrap(z, -1, NZ), core))
    to_y = ({"depth": wrap(depth, 1, ny)}, {"depth": wrap(depth, -1, ny)})
    to_sib = peer(k, 1 - core)

    def copy(src, dst, send, recv, to):
        return pltpu.make_async_remote_copy(
            src_ref=src, dst_ref=dst, send_sem=send, recv_sem=recv, device_id=to, device_id_type=MESH
        )

    def got(dst, recv):
        copy(dst, dst, recv, recv, to_sib).wait_recv()

    def sent(src, send):
        copy(src, src, send, send, to_sib).wait_send()

    barrier = pltpu.get_barrier_semaphore()
    others = [peer(wrap(k, by, NC), core_) for by in (1, 2, 3) for core_ in (0, 1)]
    partners = (*to_x, *to_z, *to_y, to_sib, *others)
    for to in partners:
        pl.semaphore_signal(barrier, inc=1, device_id=to, device_id_type=MESH)
    tokens[0, k, x, zl] = normed[...]
    tokens[1, k, x, zl] = out_grad[...]
    pl.semaphore_wait(barrier, len(partners))

    events = []

    def on(time, action, *args):
        events.append((time, len(events), functools.partial(action, *args)))

    def run():
        for _, _, action in sorted(events, key=lambda e: e[:2]):
            action()
        events.clear()

    def slot_ref(x_, slot):
        return tokens.at[:, slot // 2, x_, lax.rem(slot, 2)]

    def slot_half(x_, slot, array):
        return tokens.at[array, slot // 2, x_, lax.rem(slot, 2)]

    def tz_copy(step, way):
        slot = wrap(z, -(1 if way == 0 else -1) * (step - 1), NZ)
        ref = slot_ref(x, slot) if step < NZ // 2 else slot_half(x, slot, way)
        return copy(ref, ref, t_send.at[step - 1, way], t_recv.at[step - 1, way], to_z[way])

    offsets = (0, -1, 1, -2, 2, -3, 3, 4)

    def tx_copy(n, step, way):
        slot = wrap(z, offsets[n], NZ)
        if step == 0:
            ref = slot_ref(x, slot)
        else:
            ref = slot_half(x_left if way == 0 else x_right, slot, way)
        return copy(ref, ref, tx_send.at[n, step, way], tx_recv.at[n, step, way], to_x[way])

    def tokens_z(step):
        for way in range(2):
            if step > 1:
                slot = wrap(z, -(1 if way == 0 else -1) * (step - 1), NZ)
                full = step - 1 < NZ // 2
                got(slot_ref(x, slot) if full else slot_half(x, slot, way), t_recv.at[step - 2, way])
            if step <= NZ // 2:
                tz_copy(step, way).start()
            if 1 < step <= NZ // 2:
                for way_x in range(2):
                    tx_copy(2 * (step - 1) - 1 + way, 0, way_x).start()
        if step == 1:
            for way_x in range(2):
                tx_copy(0, 0, way_x).start()
        if step == NZ // 2 + 1:
            for way_x in range(2):
                tx_copy(7, 0, way_x).start()

    def tokens_x(n, step):
        slot = wrap(z, offsets[n], NZ)
        for way in range(2):
            if step == 1:
                got(slot_ref(x_left if way == 0 else x_right, slot), tx_recv.at[n, 0, way])
                tx_copy(n, 1, way).start()
            else:
                got(slot_half(x_far, slot, way), tx_recv.at[n, 1, way])

    def prepare():
        shift = slab.bit_length() - 1
        inner = lax.broadcasted_iota(jnp.int32, (hidden, share), 1)
        index = (inner // slab) * (hidden // ny) + lax.rem(inner, slab)
        place = lax.broadcasted_iota(jnp.int32, (hidden, share), 0)
        for h in range(2):
            perm[:, h * share : (h + 1) * share] = jnp.where(place == index + h * slab, 1.0, 0.0).astype(BF16)
        rows = hidden // ny
        mixed = dot(up_weight[pl.ds(pl.multiple_of(depth * rows, rows), rows), :], perm[...]).astype(BF16)
        for h in range(2):
            for j in range(2):
                w_own[h, 0, :, j * share : (j + 1) * share] = mixed[j * slab : (j + 1) * slab, h * share : (h + 1) * share]
            w_own[h, 1] = down_weight[pl.ds(pl.multiple_of(depth * rows + h * slab, slab), slab), :]
            to = 2 * core + h

            @pl.when(to != k)
            def _():
                for array in range(2):
                    copy(w_own.at[h, array], weights.at[array, k, depth], a_send.at[h, array], a_recv.at[k], peer(to, array)).start()

        @pl.when(core == holder)
        def _():
            for d in range(ny):
                weights[1, k, d] = down_weight[pl.ds(pl.multiple_of(d * rows + half_of * slab, slab), slab), :]
            here = pl.ds(pl.multiple_of(half_of * share, share), share)
            up_share[k] = dot(up_weight[...], perm[:, here]).astype(BF16)
            own_copies()[0].start()
            own_copies()[1].start()

    def own_copies():
        return (
            copy(weights.at[1, k], weights.at[1, k], s_send.at[3], s_recv.at[3], to_sib),
            copy(up_share.at[k], up_share.at[k], s_send.at[4], s_recv.at[4], to_sib),
        )

    def w_ref(j, slot):
        return weights.at[core, wrap(k, 1 + j, NC), slot]

    def w_half(j, slot, way):
        return weights.at[core, wrap(k, 1 + j, NC), slot, :, way * lanes : (way + 1) * lanes]

    def w_copy(j, step, way):
        slot = wrap(depth, -(1 if way == 0 else -1) * (step - 1), ny)
        ref = w_ref(j, slot) if step < ny // 2 else w_half(j, slot, way)
        return copy(ref, ref, w_send.at[j, step - 1, way], w_recv.at[j, step - 1, way], to_y[way])

    def w_sib(j):
        ref = weights.at[core, wrap(k, 1 + j, NC)]
        return copy(ref, ref, s_send.at[j], s_recv.at[j], to_sib)

    def weights_y(j, step):
        if step == 1:
            got(w_ref(j, depth), a_recv.at[wrap(k, 1 + j, NC)])
        for way in range(2):
            if step > 1:
                slot = wrap(depth, -(1 if way == 0 else -1) * (step - 1), ny)
                got(w_ref(j, slot) if step - 1 < ny // 2 else w_half(j, slot, way), w_recv.at[j, step - 2, way])
            if step <= ny // 2:
                w_copy(j, step, way).start()
        if step == ny // 2 + 1:
            w_sib(j).start()

    def weights_in(j):
        c = wrap(k, 1 + j, NC)
        got(weights.at[1 - core, c], s_recv.at[j])
        for d in range(ny):
            for i in range(2):
                base = (2 * d + i) * slab
                up_share[c, base : base + slab, :] = weights[0, c, d, :, i * share : (i + 1) * share]

    def own_in():
        @pl.when(core != holder)
        def _():
            got(weights.at[1, k], s_recv.at[3])
            got(up_share.at[k], s_recv.at[4])

        @pl.when(core == holder)
        def _():
            for one in own_copies():
                one.wait_send()

    tokens_z(1)
    prepare()
    for step in range(2, NZ // 2 + 2):
        on(3.5 * (step - 1), tokens_z, step)
    for n in range(8):
        on(3.2 * n + 4, tokens_x, n, 1)
        on(3.2 * n + 7.5, tokens_x, n, 2)
    for j in range(NC - 1):
        for step in range(1, ny // 2 + 2):
            on(5.5 + 5.5 * j + 3.4 * (step - 1), weights_y, j, step)
        on(5.5 + 5.5 * j + 3.4 * 4 + 2.5, weights_in, j)
    on(16, own_in)
    run()

    up = sum(dot(tokens[0, c].reshape(m, width), up_share[c]) for c in range(NC))
    back = sum(contract_last(tokens[1, c].reshape(m, width), weights[1, c].reshape(share, width)) for c in range(NC))
    active, slope = gelu_parts(up)
    act[...] = active.astype(BF16)
    pre_grad[...] = (back * slope).astype(BF16)

    order = tuple((dc, flip) for dc in (2, 1, 3, 0) for flip in (0, 1))

    def place(n):
        dc, flip = order[n]
        return wrap(k, dc, NC), (zl if flip == 0 else 1 - zl)

    def out_copy(n, step, way):
        c, zs = place(n)
        if step == 0:
            return copy(out.at[x_far, c, zs, way], out_half.at[n, way], x_send.at[n, 0, way], x_recv.at[n, 0, way], to_x[way])
        to_ = x_right if way == 0 else x_left
        return copy(out.at[to_, c, zs], out_full.at[n, way], x_send.at[n, 1, way], x_recv.at[n, 1, way], to_x[way])

    def grad_sib(i):
        c = wrap(k, order[2 * i][0], NC)
        return copy(grads.at[1 - core, c], grads_sib.at[c], g_send.at[i], g_recv.at[i], to_sib)

    def produce(i):
        c = wrap(k, order[2 * i][0], NC)
        branch = dot(act[...], weights[1, c].reshape(share, width)).astype(BF16)
        out[:, c, :, 0] = branch.reshape(NX, 2, block, width)
        inputs = contract_last(pre_grad[...], up_share[c]).astype(BF16)
        out[:, c, :, 1] = inputs.reshape(NX, 2, block, width)
        for n in (2 * i, 2 * i + 1):
            for way in range(2):
                out_copy(n, 0, way).start()
        down = contract_first(act[...], tokens[1, c].reshape(m, width)).astype(BF16)
        grads[1, c] = down.reshape(ny, slab, width)
        upper = contract_first(tokens[0, c].reshape(m, width), pre_grad[...]).astype(BF16)
        for d in range(ny):
            for j in range(2):
                base = (2 * d + j) * slab
                grads[0, c, d, :, j * share : (j + 1) * share] = upper[base : base + slab, :]
        grad_sib(i).start()

    for i in range(NC):
        produce(i)

    def out_x(n, step):
        c, zs = place(n)
        for way in range(2):
            out_copy(n, step - 1, way).wait_recv()
            if step == 1:
                to_ = x_right if way == 0 else x_left
                out[to_, c, zs, way] = add(out[to_, c, zs, way], out_half[n, way])
                out_copy(n, 1, way).start()
        if step == 2:
            total = out[x, c, zs].astype(F32) + out_full[n, 0].astype(F32) + out_full[n, 1].astype(F32)
            ring[2 * c + zs] = total.astype(BF16)

    def z_copy(step, way):
        slot = wrap(z, (1 if way == 0 else -1) * (NZ // 2 - step), NZ)
        if step == 0:
            return copy(ring.at[slot, way], ring_in.at[0, way, way], z_send.at[0, way], z_recv.at[0, way], to_z[way])
        return copy(ring.at[slot], ring_in.at[step, way], z_send.at[step, way], z_recv.at[step, way], to_z[way])

    def out_z(step):
        if step == NZ // 2:
            for way in range(2):
                z_copy(step - 1, way).wait_recv()
            total = ring[z].astype(F32) + ring_in[step - 1, 0].astype(F32) + ring_in[step - 1, 1].astype(F32)
            branch_out[...] = total[0].astype(BF16)
            normed_grad[...] = total[1].astype(BF16)
            return
        for way in range(2):
            slot = wrap(z, (1 if way == 0 else -1) * (NZ // 2 - step), NZ)
            if step > 0:
                z_copy(step - 1, way).wait_recv()
            if step == 1:
                ring[slot, way] = add(ring[slot, way], ring_in[0, way, way])
            elif step > 1:
                ring[slot] = add(ring[slot], ring_in[step - 1, way])
            z_copy(step, way).start()

    def y_copy(i, step, way):
        c = wrap(k, order[2 * i][0], NC)
        slot = wrap(depth, (1 if way == 0 else -1) * (ny // 2 - step), ny)
        src, dst = grads.at[core, c, slot], grads_in.at[i, step, way]
        if step == 0:
            src = grads.at[core, c, slot, :, way * lanes : (way + 1) * lanes]
            dst = grads_in.at[i, 0, way, :, way * lanes : (way + 1) * lanes]
        return copy(src, dst, y_send.at[i, step, way], y_recv.at[i, step, way], to_y[way])

    def back_copy(i):
        dc = order[2 * i][0]
        c = wrap(k, dc, NC)
        return copy(grads_own.at[i], grads_back.at[core, half_of], b_send.at[i], b_recv.at[core, half_of], peer(c, holder))

    def grads_y(i, step):
        c = wrap(k, order[2 * i][0], NC)
        if step == 0:
            got(grads_sib.at[c], g_recv.at[i])
            grads[core, c] = add(grads[core, c], grads_sib[c])
        if step < ny // 2:
            for way in range(2):
                slot = wrap(depth, (1 if way == 0 else -1) * (ny // 2 - step), ny)
                cut = slice(way * lanes, (way + 1) * lanes)
                if step > 0:
                    y_copy(i, step - 1, way).wait_recv()
                if step == 1:
                    grads[core, c, slot, :, cut] = add(grads[core, c, slot, :, cut], grads_in[i, 0, way, :, cut])
                elif step > 1:
                    grads[core, c, slot] = add(grads[core, c, slot], grads_in[i, step - 1, way])
                y_copy(i, step, way).start()
            return
        for way in range(2):
            y_copy(i, step - 1, way).wait_recv()
        total = grads[core, c, depth].astype(F32) + grads_in[i, step - 1, 0].astype(F32) + grads_in[i, step - 1, 1].astype(F32)
        grads_own[i] = total.astype(BF16)
        if order[2 * i][0] != 0:
            back_copy(i).start()
        else:
            @pl.when(core == holder)
            def _():
                grads_back[core, half_of] = grads_own[i]

            @pl.when(core != holder)
            def _():
                back_copy(i).start()

    for i in range(NC):
        for step in range(ny // 2 + 1):
            on(5 + 5.8 * i + 4 * step, grads_y, i, step)
    for n in range(8):
        on(3.5 + 3.2 * n, out_x, n, 1)
        on(8.5 + 3.2 * n, out_x, n, 2)
    on(8.6, out_z, 0)
    on(8.6 + 3.2 * 5, out_z, 1)
    on(8.7 + 3.2 * 5 + 3.5, out_z, 2)
    on(8.7 + 3.2 * 7 + 3.5, out_z, 3)
    on(8.7 + 3.2 * 7 + 7, out_z, 4)
    run()

    for h in range(2):
        for array in range(2):
            local = jnp.logical_and(2 * core + h == k, core == array)

            @pl.when(jnp.logical_not(local))
            def _():
                got(grads_back.at[array, h], b_recv.at[array, h])

    for h in range(2):
        down_grad[h * slab : (h + 1) * slab, :] = grads_back[1, h].astype(F32) * factor
    halves = [
        jnp.concatenate([grads_back[0, h, :, j * share : (j + 1) * share] for j in range(2)], axis=0) for h in range(2)
    ]
    up_grad[...] = contract_last(jnp.concatenate(halves, axis=1), perm[...]) * factor

    for way in range(2):
        for step in range(1, NZ // 2 + 1):
            tz_copy(step, way).wait_send()
        for n in range(8):
            for step in range(2):
                tx_copy(n, step, way).wait_send()
                out_copy(n, step, way).wait_send()
        for j in range(NC - 1):
            for step in range(1, ny // 2 + 1):
                w_copy(j, step, way).wait_send()
        for step in range(NZ // 2):
            z_copy(step, way).wait_send()
        for i in range(NC):
            for step in range(ny // 2):
                y_copy(i, step, way).wait_send()
    for h in range(2):
        @pl.when(2 * core + h != k)
        def _():
            for array in range(2):
                sent(w_own.at[h, array], a_send.at[h, array])
    for j in range(NC - 1):
        w_sib(j).wait_send()
    for i in range(NC):
        grad_sib(i).wait_send()
        if order[2 * i][0] != 0:
            back_copy(i).wait_send()
        else:
            @pl.when(core != holder)
            def _():
                back_copy(i).wait_send()


def solution(mesh):
    n_row, n_depth = mesh.shape["row"], mesh.shape["depth"]

    def per_device(normed, up_weight, down_weight, out_grad):
        block, width = normed.shape
        hidden = up_weight.shape[1]
        m = block * n_row // 2
        share = hidden // 2
        slab = share // n_depth
        factor = 1.0 / math.sqrt(block * n_row * n_depth)
        dma = pltpu.SemaphoreType.DMA
        vmem = pltpu.VMEM
        whole = pl.BlockSpec(memory_space=pltpu.VMEM)
        y_half = n_depth // 2
        return pl.pallas_call(
            functools.partial(kernel, (block, m, share, slab, n_depth), factor),
            out_shape=(
                jax.ShapeDtypeStruct((block, width), BF16),
                jax.ShapeDtypeStruct((block, width), BF16),
                jax.ShapeDtypeStruct((width // n_depth, hidden), F32),
                jax.ShapeDtypeStruct((hidden // n_depth, width), F32),
            ),
            in_specs=[whole] * 4,
            out_specs=[whole] * 4,
            scratch_shapes=[
                vmem((2, NC, NX, 2, block, width), BF16),
                vmem((hidden, hidden), BF16),
                vmem((2, 2, slab, width), BF16),
                vmem((2, NC, n_depth, slab, width), BF16),
                vmem((NC, width, share), BF16),
                vmem((m, share), BF16),
                vmem((m, share), BF16),
                vmem((2, NC, n_depth, slab, width), BF16),
                vmem((NC, n_depth, slab, width), BF16),
                vmem((NC, y_half, 2, slab, width), BF16),
                vmem((NC, slab, width), BF16),
                vmem((2, 2, slab, width), BF16),
                vmem((NX, NC, 2, 2, block, width), BF16),
                vmem((8, 2, block, width), BF16),
                vmem((8, 2, 2, block, width), BF16),
                vmem((NZ, 2, block, width), BF16),
                vmem((NZ // 2, 2, 2, block, width), BF16),
                dma((NZ // 2, 2)), dma((NZ // 2, 2)),
                dma((8, 2, 2)), dma((8, 2, 2)),
                dma((2, 2)), dma((NC,)),
                dma((NC - 1, y_half, 2)), dma((NC - 1, y_half, 2)),
                dma((5,)), dma((5,)),
                dma((NC,)), dma((NC,)),
                dma((NC, y_half, 2)), dma((NC, y_half, 2)),
                dma((NC,)), dma((2, 2)),
                dma((8, 2, 2)), dma((8, 2, 2)),
                dma((NZ // 2, 2)), dma((NZ // 2, 2)),
            ],
            compiler_params=pltpu.CompilerParams(
                collective_id=0, has_side_effects=True, vmem_limit_bytes=56 * 1024 * 1024
            ),
            cost_estimate=pl.CostEstimate(flops=4_000_000_000, bytes_accessed=4_000_000, transcendentals=400_000),
        )(normed, up_weight, down_weight, out_grad)

    return jax.shard_map(
        per_device,
        mesh=mesh,
        in_specs=(P(("depth", "row"), "col"), P("col", "row"), P("row", "col"), P(("depth", "row"), "col")),
        out_specs=(
            P(("depth", "row"), "col"),
            P(("depth", "row"), "col"),
            P(("col", "depth"), "row"),
            P(("row", "depth"), "col"),
        ),
        check_vma=False,
    )
```

```python
import functools
import math

import jax
import jax.numpy as jnp
from jax import lax
from jax.experimental import pallas as pl
from jax.experimental.pallas import tpu as pltpu
from jax.sharding import PartitionSpec as P

MESH = pl.DeviceIdType.MESH
BF16, F32 = jnp.bfloat16, jnp.float32
NX, NZ, NC = 4, 8, 4
PARTS = 3
ORDER = (
    ("nz", 1), ("prep",), ("own_out",), ("nz", 2), ("nx", 0, 1), ("cx", 0), ("own_in",), ("nx", 1, 1), ("nx", 2, 1),
    ("wy", 0, 1), ("nx", 0, 2), ("cx", 1), ("nx", 1, 2), ("wy", 1, 1), ("nx", 2, 2), ("wy", 0, 2), ("cx", 2),
    ("nz", 3), ("wy", 2, 1), ("cz", 0, 2), ("wy", 1, 2), ("cz", 1, 2), ("wy", 0, 3), ("cz", 2, 2), ("nx", 3, 1),
    ("cz", 3, 2), ("wy", 2, 2), ("nx", 4, 1), ("nz", 4), ("wy", 1, 3), ("cz", 0, 3), ("nx", 3, 2), ("cz", 1, 3),
    ("wy", 0, 4), ("nx", 4, 2), ("cz", 2, 3), ("nx", 5, 1), ("wy", 2, 3), ("cz", 3, 3), ("nz", 5), ("nx", 6, 1),
    ("wy", 1, 4), ("cz", 0, 4), ("wy", 0, 5), ("nx", 5, 2), ("cz", 1, 4), ("cz", 2, 4), ("wy", 2, 4), ("nx", 7, 1),
    ("w_in", 0), ("cz", 3, 4), ("wy", 1, 5), ("nx", 6, 2), ("cz", 0, 5), ("cz", 1, 5), ("cz", 2, 5), ("w_in", 1),
    ("wy", 2, 5), ("nx", 7, 2), ("cz", 3, 5), ("tok_in",), ("F", 0), ("wg", 0), ("w_in", 2), ("F", 2), ("wg", 2),
    ("gy", 0, 0), ("F", 1), ("wg", 1), ("gy", 2, 0), ("inputs",), ("gy", 0, 1), ("outputs",), ("gy", 1, 0),
    ("gy", 2, 1), ("bz", 0, 1), ("bz", 1, 1), ("bz", 2, 1), ("ox", 0, 1), ("bz", 3, 1), ("gy", 0, 2), ("ox", 1, 1),
    ("ox", 2, 1), ("gy", 1, 1), ("ox", 3, 1), ("ox", 4, 1), ("bz", 0, 2), ("ox", 5, 1), ("ox", 6, 1), ("bz", 1, 2),
    ("gy", 2, 2), ("ox", 7, 1), ("bz", 2, 2), ("ox", 0, 2), ("oz", 0), ("bz", 3, 2), ("gy", 0, 3), ("ox", 1, 2),
    ("bz", 0, 3), ("ox", 2, 2), ("bz", 1, 3), ("gy", 1, 2), ("ox", 3, 2), ("bz", 2, 3), ("ox", 4, 2), ("gy", 2, 3),
    ("ox", 5, 2), ("bz", 3, 3), ("oz", 1), ("ox", 6, 2), ("bz", 0, 4), ("gy", 0, 4), ("ox", 7, 2), ("bz", 1, 4),
    ("bz", 2, 4), ("gy", 1, 3), ("bx", 0), ("bz", 3, 4), ("oz", 2), ("gy", 2, 4), ("bx", 1), ("gy", 1, 4), ("oz", 3),
    ("oz", 4),
)


def dot(left, right):
    return jnp.dot(left, right, preferred_element_type=F32)


def contract_last(left, right):
    return lax.dot_general(left, right, (((1,), (1,)), ((), ())), preferred_element_type=F32)


def contract_first(left, right):
    return lax.dot_general(left, right, (((0,), (0,)), ((), ())), preferred_element_type=F32)


def gelu_parts(value):
    coeff = math.sqrt(2.0 / math.pi)
    square = value * value
    tangent = jnp.tanh(coeff * (value + 0.044715 * square * value))
    half = 0.5 * (1.0 + tangent)
    slope = half + 0.5 * value * (1.0 - tangent * tangent) * coeff * (1.0 + 3.0 * 0.044715 * square)
    return value * half, slope


def add(first, second):
    return (first.astype(F32) + second.astype(F32)).astype(BF16)


def wrap(index, by, size):
    return lax.rem(index + by + size, size)


def kernel(
    shape,
    normed, up_hbm, down_hbm, out_grad,
    token_sums, weight_sums,
    up_weight, down_weight, load,
    tokens, tokens_t, perm, w_own, weights, up_share,
    act, pre_grad, grads, grads_sib, grads_in, grads_own, grads_back,
    out, out_half, out_full, ring, ring_in, back, back_in, back_own, back_half, back_full,
    tz_send, tz_recv, tx_send, tx_recv, ux_send, ux_recv, uz_send, uz_recv,
    a_send, a_recv, w_send, w_recv, s_send, s_recv,
    g_send, g_recv, y_send, y_recv, b_send, b_recv,
    x_send, x_recv, z_send, z_recv, v_send, v_recv, c_send, c_recv,
):
    block, m, parts, slab, ny = shape
    width = normed.shape[1]
    hidden = up_weight.shape[1]
    w = slab * ny
    pieces = width // w
    share = parts * w
    lanes = width // 2
    row, k, depth = lax.axis_index("row"), lax.axis_index("col"), lax.axis_index("depth")
    x, zl, core = row // 4, lax.rem(row // 2, 2), lax.rem(row, 2)
    z = 2 * k + zl
    holder, half_of = k // 2, lax.rem(k, 2)

    def at(x_, z_, core_):
        return {"row": x_ * 4 + lax.rem(z_, 2) * 2 + core_, "col": z_ // 2}

    def peer(k_, core_):
        return {"row": x * 4 + zl * 2 + core_, "col": k_}

    x_right, x_left, x_far = wrap(x, 1, NX), wrap(x, -1, NX), wrap(x, 2, NX)
    to_x = (at(x_right, z, core), at(x_left, z, core))
    to_z = (at(x, wrap(z, 1, NZ), core), at(x, wrap(z, -1, NZ), core))
    to_y = ({"depth": wrap(depth, 1, ny)}, {"depth": wrap(depth, -1, ny)})
    to_sib = peer(k, 1 - core)

    def copy(src, dst, send, recv, to):
        return pltpu.make_async_remote_copy(
            src_ref=src, dst_ref=dst, send_sem=send, recv_sem=recv, device_id=to, device_id_type=MESH
        )

    def got(dst, recv):
        copy(dst, dst, recv, recv, to_sib).wait_recv()

    def sent(src, send):
        copy(src, src, send, send, to_sib).wait_send()

    def cut(way):
        return slice(way * lanes, (way + 1) * lanes)

    barrier = pltpu.get_barrier_semaphore()
    others = [peer(wrap(k, by, NC), core_) for by in (1, 2, 3) for core_ in (0, 1)]
    partners = (*to_x, *to_z, *to_y, to_sib, *others)
    for to in partners:
        pl.semaphore_signal(barrier, inc=1, device_id=to, device_id_type=MESH)
    loads = (pltpu.make_async_copy(up_hbm, up_weight, load.at[0]), pltpu.make_async_copy(down_hbm, down_weight, load.at[1]))
    for one in loads:
        one.start()
    tokens[0, k, x, zl] = normed[...]
    tokens[1, k, x, zl] = out_grad[...]
    pl.semaphore_wait(barrier, len(partners))

    def ref(array, x_, slot, way=None):
        if way is None:
            return tokens.at[array, slot // 2, x_, lax.rem(slot, 2)]
        return tokens.at[array, slot // 2, x_, lax.rem(slot, 2), :, cut(way)]

    def z_slot(step, way):
        return wrap(z, -(1 if way == 0 else -1) * step, NZ)

    def ring_copy(array, x_, step, way, send, recv):
        view = ref(array, x_, z_slot(step - 1, way), None if step < NZ // 2 else way)
        return copy(view, view, send.at[step - 1, way], recv.at[step - 1, way], to_z[way])

    def ring_got(array, x_, step, way, recv):
        got(ref(array, x_, z_slot(step, way), None if step < NZ // 2 else way), recv.at[step - 1, way])

    offsets = (0, -1, 1, -2, 2, -3, 3, 4)

    def tx_copy(n, step, way):
        slot = wrap(z, offsets[n], NZ)
        view = ref(0, x, slot) if step == 0 else ref(0, x_left if way == 0 else x_right, slot, way)
        return copy(view, view, tx_send.at[n, step, way], tx_recv.at[n, step, way], to_x[way])

    def normed_z(step):
        for way in range(2):
            if step > 1:
                ring_got(0, x, step - 1, way, tz_recv)
            if step <= NZ // 2:
                ring_copy(0, x, step, way, tz_send, tz_recv).start()
            if 1 < step <= NZ // 2:
                for way_x in range(2):
                    tx_copy(2 * (step - 1) - 1 + way, 0, way_x).start()
        if step == 1 or step == NZ // 2 + 1:
            for way_x in range(2):
                tx_copy(0 if step == 1 else 7, 0, way_x).start()

    def normed_x(n, step):
        slot = wrap(z, offsets[n], NZ)
        for way in range(2):
            if step == 1:
                got(ref(0, x_left if way == 0 else x_right, slot), tx_recv.at[n, 0, way])
                tx_copy(n, 1, way).start()
            else:
                got(ref(0, x_far, slot, way), tx_recv.at[n, 1, way])

    def ux_copy(step, way):
        view = ref(1, x, z) if step == 0 else ref(1, x_left if way == 0 else x_right, z, way)
        return copy(view, view, ux_send.at[step, way], ux_recv.at[step, way], to_x[way])

    streams = (x, x_left, x_right, x_far)

    def cotangent_x(step):
        for way in range(2):
            if step == 1:
                got(ref(1, x_left if way == 0 else x_right, z), ux_recv.at[0, way])
                ux_copy(1, way).start()
            elif step == 2:
                got(ref(1, x_far, z, way), ux_recv.at[1, way])
            else:
                ux_copy(0, way).start()
        for e in ((0,), (1, 2), (3,))[step]:
            cotangent_z(e, 1)

    def cotangent_z(e, step):
        for way in range(2):
            if step > 1:
                ring_got(1, streams[e], step - 1, way, uz_recv.at[e])
            if step <= NZ // 2:
                ring_copy(1, streams[e], step, way, uz_send.at[e], uz_recv.at[e]).start()

    rows = hidden // ny

    def pass_on(b):
        for h in range(2):
            @pl.when(2 * core + h != k)
            def _():
                for array in range(2):
                    pass_copy(array, b, h).start()

    def pass_copy(array, b, h):
        to = 2 * core + h
        there = lax.rem(k - to + NC - 1, NC)
        return copy(
            w_own.at[h, array, b], weights.at[array, b, depth, there],
            a_send.at[h, array, b], a_recv.at[b, there], peer(to, array),
        )

    def prepare():
        for one in loads:
            one.wait()
        for h in range(2):
            for b in range(parts):
                w_own[h, 1, b] = down_weight[pl.ds(pl.multiple_of(depth * rows + (h * parts + b) * slab, slab), slab), :]
        inner = lax.broadcasted_iota(jnp.int32, (hidden, w), 1)
        index = (inner // slab) * rows + lax.rem(inner, slab)
        index = lax.broadcasted_iota(jnp.int32, (hidden, w), 0) - index
        for g in range(2 * parts):
            perm[:, g * w : (g + 1) * w] = jnp.where(index == g * slab, 1.0, 0.0).astype(BF16)
        mixed = dot(up_weight[pl.ds(pl.multiple_of(depth * rows, rows), rows), :], perm[...]).astype(BF16)
        for h in range(2):
            for b in range(parts):
                g = h * parts + b
                for i in range(pieces):
                    w_own[h, 0, b, :, i * w : (i + 1) * w] = mixed[i * slab : (i + 1) * slab, g * w : (g + 1) * w]
        for b in range(parts):
            pass_on(b)

    def own_copies():
        return (
            copy(weights.at[1, :, :, NC - 1], weights.at[1, :, :, NC - 1], s_send.at[parts], s_recv.at[parts], to_sib),
            copy(up_share.at[:, NC - 1], up_share.at[:, NC - 1], s_send.at[parts + 1], s_recv.at[parts + 1], to_sib),
        )

    def own_out():
        @pl.when(core == holder)
        def _():
            for b in range(parts):
                for d in range(ny):
                    base = d * rows + half_of * (parts * slab) + b * slab
                    weights[1, b, d, NC - 1] = down_weight[pl.ds(pl.multiple_of(base, slab), slab), :]
            here = pl.ds(pl.multiple_of(half_of * share, share), share)
            up_own = dot(up_weight[...], perm[:, here]).astype(BF16)
            for b in range(parts):
                up_share[b, NC - 1] = up_own[:, b * w : (b + 1) * w]
            for one in own_copies():
                one.start()

    def own_in():
        @pl.when(core != holder)
        def _():
            got(weights.at[1, :, :, NC - 1], s_recv.at[parts])
            got(up_share.at[:, NC - 1], s_recv.at[parts + 1])

    def w_ref(b, step, way):
        slot = wrap(depth, -(1 if way == 0 else -1) * step, ny)
        if step < ny // 2:
            return weights.at[core, b, slot, 0 : NC - 1]
        return weights.at[core, b, slot, 0 : NC - 1, :, cut(way)]

    def w_copy(b, step, way):
        slot = wrap(depth, -(1 if way == 0 else -1) * (step - 1), ny)
        view = weights.at[core, b, slot, 0 : NC - 1]
        if step == ny // 2:
            view = weights.at[core, b, slot, 0 : NC - 1, :, cut(way)]
        return copy(view, view, w_send.at[b, step - 1, way], w_recv.at[b, step - 1, way], to_y[way])

    def w_sib(b):
        view = weights.at[core, b, :, 0 : NC - 1]
        return copy(view, view, s_send.at[b], s_recv.at[b], to_sib)

    def weights_y(b, step):
        if step == 1:
            for there in range(NC - 1):
                got(weights.at[core, b, depth, there], a_recv.at[b, there])
        for way in range(2):
            if step > 1:
                got(w_ref(b, step - 1, way), w_recv.at[b, step - 2, way])
            if step <= ny // 2:
                w_copy(b, step, way).start()
        if step == ny // 2 + 1:
            w_sib(b).start()

    def weights_in(b):
        got(weights.at[1 - core, b, :, 0 : NC - 1], s_recv.at[b])
        for there in range(NC - 1):
            for d in range(ny):
                for i in range(pieces):
                    base = (pieces * d + i) * slab
                    up_share[b, there, base : base + slab, :] = weights[0, b, d, there, :, i * w : (i + 1) * w]

    def feature(there):
        return wrap(k, 1 + there, NC)

    def tokens_in():
        for c in range(NC):
            tokens_t[c] = tokens[0, c].reshape(m, width).T

    def down_share(b, there):
        return weights[1, b, :, there].reshape(w, width)

    def forward(b):
        up = sum(dot(tokens[0, feature(i)].reshape(m, width), up_share[b, i]) for i in range(NC))
        cotangent = sum(contract_last(tokens[1, feature(i)].reshape(m, width), down_share(b, i)) for i in range(NC))
        active, slope = gelu_parts(up)
        act[b] = active.astype(BF16)
        pre_grad[b] = (cotangent * slope).astype(BF16)

    def grad_sib(b):
        return copy(grads.at[1 - core, b], grads_sib.at[b], g_send.at[b], g_recv.at[b], to_sib)

    def weight_grads(b):
        for i in range(NC):
            c = feature(i)
            down = contract_first(act[b], tokens[1, c].reshape(m, width)).astype(BF16)
            grads[1, b, :, i] = down.reshape(ny, slab, width)
            upper = dot(tokens_t[c], pre_grad[b]).astype(BF16)
            for d in range(ny):
                for j in range(pieces):
                    base = (pieces * d + j) * slab
                    grads[0, b, d, i, :, j * w : (j + 1) * w] = upper[base : base + slab, :]
        grad_sib(b).start()

    def y_copy(b, step, way):
        slot = wrap(depth, (1 if way == 0 else -1) * (ny // 2 - step), ny)
        src, dst = grads.at[core, b, slot], grads_in.at[b, step, way]
        if step == 0:
            some = slice(2 * way, 2 * way + 2)
            src, dst = grads.at[core, b, slot, some], grads_in.at[b, 0, way, some]
        return copy(src, dst, y_send.at[b, step, way], y_recv.at[b, step, way], to_y[way])

    def back_copy(b, there):
        return copy(
            grads_own.at[b, there], grads_back.at[core, half_of, b],
            b_send.at[b, there], b_recv.at[core, half_of, b], peer(feature(there), holder),
        )

    def grads_y(b, step):
        if step == 0:
            got(grads_sib.at[b], g_recv.at[b])
            grads[core, b] = add(grads[core, b], grads_sib[b])
        if step < ny // 2:
            for way in range(2):
                slot = wrap(depth, (1 if way == 0 else -1) * (ny // 2 - step), ny)
                some = slice(2 * way, 2 * way + 2)
                if step > 0:
                    y_copy(b, step - 1, way).wait_recv()
                if step == 1:
                    grads[core, b, slot, some] = add(grads[core, b, slot, some], grads_in[b, 0, way, some])
                elif step > 1:
                    grads[core, b, slot] = add(grads[core, b, slot], grads_in[b, step - 1, way])
                y_copy(b, step, way).start()
            return
        for way in range(2):
            y_copy(b, step - 1, way).wait_recv()
        total = grads[core, b, depth].astype(F32) + grads_in[b, step - 1, 0].astype(F32) + grads_in[b, step - 1, 1].astype(F32)
        grads_own[b] = total.astype(BF16)
        for there in range(NC - 1):
            back_copy(b, there).start()

        @pl.when(core == holder)
        def _():
            grads_back[core, half_of, b] = grads_own[b, NC - 1]

        @pl.when(core != holder)
        def _():
            back_copy(b, NC - 1).start()

    targets = (x_far, x_right, x_left, x)

    def back_ref(e, step, way):
        slot = wrap(z, (1 if way == 0 else -1) * (NZ // 2 - step), NZ)
        index = (targets[e], slot // 2, lax.rem(slot, 2))
        return (*index, slice(None), cut(way)) if step == 0 else index

    def back_z_copy(e, step, way):
        dst = (e, 0, way, slice(None), cut(way)) if step == 0 else (e, step, way)
        return copy(back.at[back_ref(e, step, way)], back_in.at[dst], v_send.at[e, step, way], v_recv.at[e, step, way], to_z[way])

    def back_x_copy(step, way):
        if step == 0:
            src, dst = back_own.at[0, :, cut(way)], back_half.at[way, :, cut(way)]
        else:
            src, dst = back_own.at[1 + way], back_full.at[way]
        return copy(src, dst, c_send.at[step, way], c_recv.at[step, way], to_x[way])

    def inputs():
        cotangent = jnp.concatenate([pre_grad[b] for b in range(parts)], axis=1)
        for i in range(NC):
            weight = jnp.concatenate([up_share[b, i] for b in range(parts)], axis=1)
            back[:, feature(i)] = contract_last(cotangent, weight).astype(BF16).reshape(NX, 2, block, width)
        for e in range(NX):
            for way in range(2):
                back_z_copy(e, 0, way).start()

    def back_z(e, step):
        if step < NZ // 2:
            for way in range(2):
                back_z_copy(e, step - 1, way).wait_recv()
                index = back_ref(e, step, way)
                if step == 1:
                    index = (*index, slice(None), cut(way))
                    back[index] = add(back[index], back_in[e, 0, way, :, cut(way)])
                else:
                    back[index] = add(back[index], back_in[e, step - 1, way])
                back_z_copy(e, step, way).start()
            return
        for way in range(2):
            back_z_copy(e, step - 1, way).wait_recv()
        total = back[targets[e], k, zl].astype(F32) + back_in[e, step - 1, 0].astype(F32) + back_in[e, step - 1, 1].astype(F32)
        back_own[e] = total.astype(BF16)
        if e == 0:
            for way in range(2):
                back_x_copy(0, way).start()

    def back_x(step):
        for way in range(2):
            back_x_copy(step, way).wait_recv()
            if step == 0:
                back_own[1 + way, :, cut(way)] = add(back_own[1 + way, :, cut(way)], back_half[way, :, cut(way)])
                back_x_copy(1, way).start()
        if step == 1:
            total = back_own[3].astype(F32) + back_full[0].astype(F32) + back_full[1].astype(F32)
            token_sums[1] = total.astype(BF16)

    order = tuple((dc, flip) for dc in (2, 1, 3, 0) for flip in (0, 1))

    def place(n):
        dc, flip = order[n]
        return wrap(k, dc, NC), (zl if flip == 0 else 1 - zl)

    def out_copy(n, step, way):
        c, zs = place(n)
        if step == 0:
            src, dst = out.at[x_far, c, zs, :, cut(way)], out_half.at[n, way, :, cut(way)]
        else:
            src, dst = out.at[x_right if way == 0 else x_left, c, zs], out_full.at[n, way]
        return copy(src, dst, x_send.at[n, step, way], x_recv.at[n, step, way], to_x[way])

    def outputs():
        active = jnp.concatenate([act[b] for b in range(parts)], axis=1)
        for i in range(NC):
            dc = order[2 * i][0]
            there = (dc - 1) % NC
            weight = jnp.concatenate([down_share(b, there) for b in range(parts)], axis=0)
            out[:, feature(there)] = dot(active, weight).astype(BF16).reshape(NX, 2, block, width)
            for n in (2 * i, 2 * i + 1):
                for way in range(2):
                    out_copy(n, 0, way).start()

    def out_x(n, step):
        c, zs = place(n)
        for way in range(2):
            out_copy(n, step - 1, way).wait_recv()
            if step == 1:
                to_ = x_right if way == 0 else x_left
                out[to_, c, zs, :, cut(way)] = add(out[to_, c, zs, :, cut(way)], out_half[n, way, :, cut(way)])
                out_copy(n, 1, way).start()
        if step == 2:
            total = out[x, c, zs].astype(F32) + out_full[n, 0].astype(F32) + out_full[n, 1].astype(F32)
            ring[2 * c + zs] = total.astype(BF16)

    def z_copy(step, way):
        slot = wrap(z, (1 if way == 0 else -1) * (NZ // 2 - step), NZ)
        src, dst = ring.at[slot], ring_in.at[step, way]
        if step == 0:
            src, dst = ring.at[slot, :, cut(way)], ring_in.at[0, way, :, cut(way)]
        return copy(src, dst, z_send.at[step, way], z_recv.at[step, way], to_z[way])

    def out_z(step):
        if step == NZ // 2:
            for way in range(2):
                z_copy(step - 1, way).wait_recv()
            total = ring[z].astype(F32) + ring_in[step - 1, 0].astype(F32) + ring_in[step - 1, 1].astype(F32)
            token_sums[0] = total.astype(BF16)
            return
        for way in range(2):
            slot = wrap(z, (1 if way == 0 else -1) * (NZ // 2 - step), NZ)
            if step > 0:
                z_copy(step - 1, way).wait_recv()
            if step == 1:
                ring[slot, :, cut(way)] = add(ring[slot, :, cut(way)], ring_in[0, way, :, cut(way)])
            elif step > 1:
                ring[slot] = add(ring[slot], ring_in[step - 1, way])
            z_copy(step, way).start()

    steps = dict(
        cx=cotangent_x, cz=cotangent_z, nz=normed_z, nx=normed_x, prep=prepare, own_out=own_out, own_in=own_in,
        wy=weights_y, w_in=weights_in, tok_in=tokens_in, F=forward, wg=weight_grads, gy=grads_y,
        inputs=inputs, outputs=outputs, bz=back_z, bx=back_x, ox=out_x, oz=out_z,
    )
    for name, *index in ORDER:
        steps[name](*index)

    for h in range(2):
        for array in range(2):
            local = jnp.logical_and(2 * core + h == k, core == array)

            @pl.when(jnp.logical_not(local))
            def _():
                for b in range(parts):
                    got(grads_back.at[array, h, b], b_recv.at[array, h, b])

    for h in range(2):
        for b in range(parts):
            base = (h * parts + b) * slab
            weight_sums[1, base : base + slab, :] = grads_back[1, h, b]
    columns = [
        jnp.concatenate([grads_back[0, h, b, :, i * w : (i + 1) * w] for i in range(pieces)], axis=0)
        for h in range(2) for b in range(parts)
    ]
    weight_sums[0] = contract_last(jnp.concatenate(columns, axis=1), perm[...]).astype(BF16)

    for way in range(2):
        for step in range(1, NZ // 2 + 1):
            ring_copy(0, x, step, way, tz_send, tz_recv).wait_send()
            for e in range(4):
                ring_copy(1, streams[e], step, way, uz_send.at[e], uz_recv.at[e]).wait_send()
                back_z_copy(e, step - 1, way).wait_send()
            z_copy(step - 1, way).wait_send()
        for step in range(2):
            for n in range(8):
                tx_copy(n, step, way).wait_send()
                out_copy(n, step, way).wait_send()
            ux_copy(step, way).wait_send()
            back_x_copy(step, way).wait_send()
        for b in range(parts):
            for step in range(1, ny // 2 + 1):
                w_copy(b, step, way).wait_send()
                y_copy(b, step - 1, way).wait_send()
    for h in range(2):
        @pl.when(2 * core + h != k)
        def _():
            for array in range(2):
                for b in range(parts):
                    pass_copy(array, b, h).wait_send()
    for b in range(parts):
        w_sib(b).wait_send()
        grad_sib(b).wait_send()
        for there in range(NC - 1):
            back_copy(b, there).wait_send()

        @pl.when(core != holder)
        def _():
            back_copy(b, NC - 1).wait_send()

    @pl.when(core == holder)
    def _():
        for one in own_copies():
            one.wait_send()


def solution(mesh):
    n_row, n_depth = mesh.shape["row"], mesh.shape["depth"]

    def per_device(normed, up_weight, down_weight, out_grad):
        block, width = normed.shape
        hidden = up_weight.shape[1]
        m = block * n_row // 2
        parts = PARTS
        slab = hidden // 2 // parts // n_depth
        w = slab * n_depth
        factor = 1.0 / math.sqrt(block * n_row * n_depth)
        dma = pltpu.SemaphoreType.DMA
        vmem = pltpu.VMEM
        whole = pl.BlockSpec(memory_space=pltpu.VMEM)
        y_half = n_depth // 2
        token_sums, weight_sums = pl.pallas_call(
            functools.partial(kernel, (block, m, parts, slab, n_depth)),
            out_shape=(
                jax.ShapeDtypeStruct((2, block, width), BF16),
                jax.ShapeDtypeStruct((2, hidden // n_depth, width), BF16),
            ),
            in_specs=[whole, pl.BlockSpec(memory_space=pl.ANY), pl.BlockSpec(memory_space=pl.ANY), whole],
            out_specs=[whole] * 2,
            scratch_shapes=[
                vmem((width, hidden), BF16),
                vmem((hidden, width), BF16),
                dma((2,)),
                vmem((2, NC, NX, 2, block, width), BF16),
                vmem((NC, width, m), BF16),
                vmem((hidden, hidden), BF16),
                vmem((2, 2, parts, slab, width), BF16),
                vmem((2, parts, n_depth, NC, slab, width), BF16),
                vmem((parts, NC, width, w), BF16),
                vmem((parts, m, w), BF16),
                vmem((parts, m, w), BF16),
                vmem((2, parts, n_depth, NC, slab, width), BF16),
                vmem((parts, n_depth, NC, slab, width), BF16),
                vmem((parts, y_half, 2, NC, slab, width), BF16),
                vmem((parts, NC, slab, width), BF16),
                vmem((2, 2, parts, slab, width), BF16),
                vmem((NX, NC, 2, block, width), BF16),
                vmem((8, 2, block, width), BF16),
                vmem((8, 2, block, width), BF16),
                vmem((NZ, block, width), BF16),
                vmem((NZ // 2, 2, block, width), BF16),
                vmem((NX, NC, 2, block, width), BF16),
                vmem((NX, NZ // 2, 2, block, width), BF16),
                vmem((NX, block, width), BF16),
                vmem((2, block, width), BF16),
                vmem((2, block, width), BF16),
                dma((NZ // 2, 2)), dma((NZ // 2, 2)),
                dma((8, 2, 2)), dma((8, 2, 2)),
                dma((2, 2)), dma((2, 2)),
                dma((NX, NZ // 2, 2)), dma((NX, NZ // 2, 2)),
                dma((2, 2, parts)), dma((parts, NC - 1)),
                dma((parts, y_half, 2)), dma((parts, y_half, 2)),
                dma((parts + 2,)), dma((parts + 2,)),
                dma((parts,)), dma((parts,)),
                dma((parts, y_half, 2)), dma((parts, y_half, 2)),
                dma((parts, NC)), dma((2, 2, parts)),
                dma((8, 2, 2)), dma((8, 2, 2)),
                dma((NZ // 2, 2)), dma((NZ // 2, 2)),
                dma((NX, NZ // 2, 2)), dma((NX, NZ // 2, 2)),
                dma((2, 2)), dma((2, 2)),
            ],
            compiler_params=pltpu.CompilerParams(
                collective_id=0, has_side_effects=True, vmem_limit_bytes=56 * 1024 * 1024
            ),
            cost_estimate=pl.CostEstimate(flops=4_000_000_000, bytes_accessed=4_000_000, transcendentals=400_000),
        )(normed, up_weight, down_weight, out_grad)
        up_grad, down_grad = weight_sums[0].astype(F32) * factor, weight_sums[1].astype(F32) * factor
        return token_sums[0], token_sums[1], up_grad, down_grad

    return jax.shard_map(
        per_device,
        mesh=mesh,
        in_specs=(P(("depth", "row"), "col"), P("col", "row"), P("row", "col"), P(("depth", "row"), "col")),
        out_specs=(
            P(("depth", "row"), "col"),
            P(("depth", "row"), "col"),
            P(("col", "depth"), "row"),
            P(("row", "depth"), "col"),
        ),
        check_vma=False,
    )
```

```python
import functools
import math

import jax
import jax.numpy as jnp
from jax import lax
from jax.experimental import pallas as pl
from jax.experimental.pallas import tpu as pltpu
from jax.sharding import PartitionSpec as P

MESH = pl.DeviceIdType.MESH
BF16, F32 = jnp.bfloat16, jnp.float32
NX, NZ, NC = 4, 8, 4
PARTS = 3
ORDER = (
    ("nz", 1), ("cx", 0), ("prep",), ("own_out",), ("nz", 2), ("nx", 0, 1), ("cx", 1), ("cz", 0, 2), ("own_in",),
    ("wy", 0, 1), ("nx", 1, 1), ("wy", 1, 1), ("nx", 2, 1), ("nx", 0, 2), ("cx", 2), ("wy", 2, 1), ("nx", 1, 2),
    ("wy", 0, 2), ("nz", 3), ("cz", 1, 2), ("nx", 2, 2), ("cz", 2, 2), ("wy", 1, 2), ("cz", 0, 3), ("cz", 3, 2),
    ("wy", 2, 2), ("nx", 3, 1), ("nz", 4), ("cz", 1, 3), ("wy", 0, 3), ("cz", 2, 3), ("nx", 4, 1), ("cz", 0, 4),
    ("wy", 1, 3), ("cz", 3, 3), ("nx", 3, 2), ("nz", 5), ("wy", 2, 3), ("cz", 1, 4), ("nx", 5, 1), ("cz", 2, 4),
    ("cz", 0, 5), ("wy", 0, 4), ("nx", 6, 1), ("cz", 3, 4), ("nx", 4, 2), ("wy", 1, 4), ("cz", 1, 5), ("cz", 2, 5),
    ("nx", 7, 1), ("wy", 2, 4), ("nx", 5, 2), ("wy", 0, 5), ("cz", 3, 5), ("nx", 6, 2), ("wy", 1, 5), ("w_in", 0),
    ("nx", 7, 2), ("tok_in",), ("wy", 2, 5), ("F", 0), ("wg", 0), ("w_in", 2), ("F", 2), ("wg", 2), ("gy", 0, 0, 1),
    ("gy", 0, 0, 0), ("w_in", 1), ("F", 1), ("wg", 1), ("gy", 2, 0, 0), ("inputs",), ("gy", 0, 1, 0), ("gy", 0, 1, 1),
    ("outputs",), ("gy", 1, 0, 0), ("gy", 1, 0, 1), ("gy", 2, 0, 1), ("gy", 2, 1, 0), ("bz", 0, 1), ("bz", 1, 1),
    ("gy", 0, 2, 0), ("drain",), ("bz", 2, 1), ("ox", 0, 1), ("bz", 3, 1), ("gy", 0, 2, 1), ("ox", 1, 1),
    ("gy", 1, 1, 0), ("ox", 2, 1), ("gy", 1, 1, 1), ("ox", 3, 1), ("gy", 2, 1, 1), ("ox", 4, 1), ("bz", 0, 2),
    ("ox", 5, 1), ("gy", 2, 2, 0), ("ox", 6, 1), ("bz", 1, 2), ("ox", 7, 1), ("gy", 0, 3, 0), ("bz", 2, 2),
    ("ox", 0, 2), ("oz", 0), ("gy", 0, 3, 1), ("bz", 3, 2), ("ox", 1, 2), ("gy", 1, 2, 0), ("bz", 0, 3), ("ox", 2, 2),
    ("gy", 1, 2, 1), ("bz", 1, 3), ("ox", 3, 2), ("gy", 2, 2, 1), ("bz", 2, 3), ("ox", 4, 2), ("gy", 2, 3, 0),
    ("ox", 5, 2), ("oz", 1), ("gy", 0, 4, 0), ("bz", 3, 3), ("ox", 6, 2), ("gy", 0, 4, 1), ("bz", 0, 4), ("ox", 7, 2),
    ("gy", 1, 3, 0), ("bz", 1, 4), ("gy", 1, 3, 1), ("bz", 2, 4), ("gy", 2, 3, 1), ("oz", 2), ("bx", 0),
    ("gy", 2, 4, 0), ("gy", 1, 4, 0), ("bz", 3, 4), ("gy", 1, 4, 1), ("gy", 2, 4, 1), ("bx", 1), ("oz", 3), ("oz", 4),
)
FIRST = 2


def dot(left, right):
    return jnp.dot(left, right, preferred_element_type=F32)


def contract_last(left, right):
    return lax.dot_general(left, right, (((1,), (1,)), ((), ())), preferred_element_type=F32)


def contract_first(left, right):
    return lax.dot_general(left, right, (((0,), (0,)), ((), ())), preferred_element_type=F32)


def gelu_parts(value):
    coeff = math.sqrt(2.0 / math.pi)
    square = value * value
    tangent = jnp.tanh(coeff * (value + 0.044715 * square * value))
    half = 0.5 * (1.0 + tangent)
    slope = half + 0.5 * value * (1.0 - tangent * tangent) * coeff * (1.0 + 3.0 * 0.044715 * square)
    return value * half, slope


def add(first, second):
    return (first.astype(F32) + second.astype(F32)).astype(BF16)


def wrap(index, by, size):
    return lax.rem(index + by + size, size)


def kernel(
    shape,
    normed, up_hbm, down_hbm, out_grad,
    token_sums, weight_sums,
    up_weight, down_weight, load,
    tokens, tokens_t, perm, w_own, weights, up_share,
    act, pre_grad, grads, grads_sib, grads_in, grads_own, grads_back,
    out, out_half, out_full, ring, ring_in, back, back_in, back_own, back_half, back_full,
    tz_send, tz_recv, tx_send, tx_recv, ux_send, ux_recv, uz_send, uz_recv,
    a_send, a_recv, w_send, w_recv, s_send, s_recv,
    g_send, g_recv, y_send, y_recv, b_send, b_recv,
    x_send, x_recv, z_send, z_recv, v_send, v_recv, c_send, c_recv,
):
    block, m, parts, slab, ny = shape
    width = normed.shape[1]
    hidden = up_weight.shape[1]
    w = slab * ny
    pieces = width // w
    share = parts * w
    lanes = width // 2
    first = FIRST * w
    row, k, depth = lax.axis_index("row"), lax.axis_index("col"), lax.axis_index("depth")
    x, zl, core = row // 4, lax.rem(row // 2, 2), lax.rem(row, 2)
    z = 2 * k + zl
    holder, half_of = k // 2, lax.rem(k, 2)

    def at(x_, z_, core_):
        return {"row": x_ * 4 + lax.rem(z_, 2) * 2 + core_, "col": z_ // 2}

    def peer(k_, core_):
        return {"row": x * 4 + zl * 2 + core_, "col": k_}

    x_right, x_left, x_far = wrap(x, 1, NX), wrap(x, -1, NX), wrap(x, 2, NX)
    to_x = (at(x_right, z, core), at(x_left, z, core))
    to_z = (at(x, wrap(z, 1, NZ), core), at(x, wrap(z, -1, NZ), core))
    to_y = ({"depth": wrap(depth, 1, ny)}, {"depth": wrap(depth, -1, ny)})
    to_sib = peer(k, 1 - core)

    def copy(src, dst, send, recv, to):
        return pltpu.make_async_remote_copy(
            src_ref=src, dst_ref=dst, send_sem=send, recv_sem=recv, device_id=to, device_id_type=MESH
        )

    def got(dst, recv):
        copy(dst, dst, recv, recv, to_sib).wait_recv()

    def sent(src, send):
        copy(src, src, send, send, to_sib).wait_send()

    def cut(way):
        return slice(way * (block // 2), (way + 1) * (block // 2))

    def lane_cut(way):
        return slice(way * lanes, (way + 1) * lanes)

    barrier = pltpu.get_barrier_semaphore()
    others = [peer(wrap(k, by, NC), core_) for by in (1, 2, 3) for core_ in (0, 1)]
    partners = (*to_x, *to_z, *to_y, to_sib, *others)
    for to in partners:
        pl.semaphore_signal(barrier, inc=1, device_id=to, device_id_type=MESH)
    loads = (pltpu.make_async_copy(up_hbm, up_weight, load.at[0]), pltpu.make_async_copy(down_hbm, down_weight, load.at[1]))
    for one in loads:
        one.start()
    tokens[0, k, x, zl] = normed[...]
    tokens[1, k, x, zl] = out_grad[...]
    pl.semaphore_wait(barrier, len(partners))

    segments = ((0, slice(0, width)), (1, slice(0, first)), (1, slice(first, width)))

    def ref(segment, x_, slot, way=None):
        array, columns = segments[segment]
        return tokens.at[array, slot // 2, x_, lax.rem(slot, 2), slice(0, block) if way is None else cut(way), columns]

    def z_slot(step, way):
        return wrap(z, -(1 if way == 0 else -1) * step, NZ)

    def ring_copy(segment, x_, step, way, send, recv):
        view = ref(segment, x_, z_slot(step - 1, way), None if step < NZ // 2 else way)
        return copy(view, view, send.at[step - 1, way], recv.at[step - 1, way], to_z[way])

    def ring_got(segment, x_, step, way, recv):
        got(ref(segment, x_, z_slot(step, way), None if step < NZ // 2 else way), recv.at[step - 1, way])

    offsets = (0, -1, 1, -2, 2, -3, 3, 4)

    def tz_copy(g, step, way):
        return ring_copy(g, x, step, way, tz_send.at[g], tz_recv.at[g])

    def tx_copy(g, n, step, way):
        slot = wrap(z, offsets[n], NZ)
        view = ref(g, x, slot) if step == 0 else ref(g, x_left if way == 0 else x_right, slot, way)
        return copy(view, view, tx_send.at[g, n, step, way], tx_recv.at[g, n, step, way], to_x[way])

    def normed_z(step):
        for way in range(2):
            for g in range(2):
                if step > 1:
                    ring_got(g, x, step - 1, way, tz_recv.at[g])
                if step <= NZ // 2:
                    tz_copy(g, step, way).start()
            if 1 < step <= NZ // 2:
                for way_x in range(2):
                    for g in range(2):
                        tx_copy(g, 2 * (step - 1) - 1 + way, 0, way_x).start()
        if step == 1 or step == NZ // 2 + 1:
            for way_x in range(2):
                for g in range(2):
                    tx_copy(g, 0 if step == 1 else 7, 0, way_x).start()

    def normed_x(n, step):
        slot = wrap(z, offsets[n], NZ)
        for way in range(2):
            for g in range(2):
                if step == 1:
                    got(ref(g, x_left if way == 0 else x_right, slot), tx_recv.at[g, n, 0, way])
                    tx_copy(g, n, 1, way).start()
                else:
                    got(ref(g, x_far, slot, way), tx_recv.at[g, n, 1, way])

    def ux_copy(step, way):
        view = ref(2, x, z) if step == 0 else ref(2, x_left if way == 0 else x_right, z, way)
        return copy(view, view, ux_send.at[step, way], ux_recv.at[step, way], to_x[way])

    streams = (x, x_left, x_right, x_far)

    def cotangent_x(step):
        for way in range(2):
            if step == 1:
                got(ref(2, x_left if way == 0 else x_right, z), ux_recv.at[0, way])
                ux_copy(1, way).start()
            elif step == 2:
                got(ref(2, x_far, z, way), ux_recv.at[1, way])
            else:
                ux_copy(0, way).start()
        for e in ((0,), (1, 2), (3,))[step]:
            cotangent_z(e, 1)

    def cotangent_z(e, step):
        for way in range(2):
            if step > 1:
                ring_got(2, streams[e], step - 1, way, uz_recv.at[e])
            if step <= NZ // 2:
                ring_copy(2, streams[e], step, way, uz_send.at[e], uz_recv.at[e]).start()

    rows = hidden // ny

    def pass_on(b):
        for h in range(2):
            @pl.when(2 * core + h != k)
            def _():
                for array in range(2):
                    pass_copy(array, b, h).start()

    def pass_copy(array, b, h):
        to = 2 * core + h
        there = lax.rem(k - to + NC - 1, NC)
        return copy(
            w_own.at[h, array, b], weights.at[array, b, depth, there],
            a_send.at[h, array, b], a_recv.at[b, there], peer(to, array),
        )

    def prepare():
        for one in loads:
            one.wait()
        for h in range(2):
            for b in range(parts):
                w_own[h, 1, b] = down_weight[pl.ds(pl.multiple_of(depth * rows + (h * parts + b) * slab, slab), slab), :]
        inner = lax.broadcasted_iota(jnp.int32, (hidden, w), 1)
        index = (inner // slab) * rows + lax.rem(inner, slab)
        index = lax.broadcasted_iota(jnp.int32, (hidden, w), 0) - index
        for g in range(2 * parts):
            perm[:, g * w : (g + 1) * w] = jnp.where(index == g * slab, 1.0, 0.0).astype(BF16)
        mixed = dot(up_weight[pl.ds(pl.multiple_of(depth * rows, rows), rows), :], perm[...]).astype(BF16)
        for h in range(2):
            for b in range(parts):
                g = h * parts + b
                for i in range(pieces):
                    w_own[h, 0, b, :, i * w : (i + 1) * w] = mixed[i * slab : (i + 1) * slab, g * w : (g + 1) * w]
        for b in range(parts):
            pass_on(b)

    def own_copies():
        return (
            copy(weights.at[1, :, :, NC - 1], weights.at[1, :, :, NC - 1], s_send.at[parts], s_recv.at[parts], to_sib),
            copy(up_share.at[:, NC - 1], up_share.at[:, NC - 1], s_send.at[parts + 1], s_recv.at[parts + 1], to_sib),
        )

    def own_out():
        @pl.when(core == holder)
        def _():
            for b in range(parts):
                for d in range(ny):
                    base = d * rows + half_of * (parts * slab) + b * slab
                    weights[1, b, d, NC - 1] = down_weight[pl.ds(pl.multiple_of(base, slab), slab), :]
            here = pl.ds(pl.multiple_of(half_of * share, share), share)
            up_own = dot(up_weight[...], perm[:, here]).astype(BF16)
            for b in range(parts):
                up_share[b, NC - 1] = up_own[:, b * w : (b + 1) * w]
            for one in own_copies():
                one.start()

    def own_in():
        @pl.when(core != holder)
        def _():
            got(weights.at[1, :, :, NC - 1], s_recv.at[parts])
            got(up_share.at[:, NC - 1], s_recv.at[parts + 1])

    def w_ref(b, step, way):
        slot = wrap(depth, -(1 if way == 0 else -1) * step, ny)
        if step < ny // 2:
            return weights.at[core, b, slot, 0 : NC - 1]
        return weights.at[core, b, slot, 0 : NC - 1, :, lane_cut(way)]

    def w_copy(b, step, way):
        slot = wrap(depth, -(1 if way == 0 else -1) * (step - 1), ny)
        view = weights.at[core, b, slot, 0 : NC - 1]
        if step == ny // 2:
            view = weights.at[core, b, slot, 0 : NC - 1, :, lane_cut(way)]
        return copy(view, view, w_send.at[b, step - 1, way], w_recv.at[b, step - 1, way], to_y[way])

    def w_sib(b):
        view = weights.at[core, b, :, 0 : NC - 1]
        return copy(view, view, s_send.at[b], s_recv.at[b], to_sib)

    def weights_y(b, step):
        if step == 1:
            for there in range(NC - 1):
                got(weights.at[core, b, depth, there], a_recv.at[b, there])
        for way in range(2):
            if step > 1:
                got(w_ref(b, step - 1, way), w_recv.at[b, step - 2, way])
            if step <= ny // 2:
                w_copy(b, step, way).start()
        if step == ny // 2 + 1:
            w_sib(b).start()

    def weights_in(b):
        got(weights.at[1 - core, b, :, 0 : NC - 1], s_recv.at[b])
        for there in range(NC - 1):
            for d in range(ny):
                for i in range(pieces):
                    base = (pieces * d + i) * slab
                    up_share[b, there, base : base + slab, :] = weights[0, b, d, there, :, i * w : (i + 1) * w]

    def feature(there):
        return wrap(k, 1 + there, NC)

    def tokens_in():
        for c in range(NC):
            tokens_t[c] = tokens[0, c].reshape(m, width).T

    def down_share(b, there):
        return weights[1, b, :, there].reshape(w, width)

    def forward(b):
        up = sum(dot(tokens[0, feature(i)].reshape(m, width), up_share[b, i]) for i in range(NC))
        cotangent = sum(contract_last(tokens[1, feature(i)].reshape(m, width), down_share(b, i)) for i in range(NC))
        active, slope = gelu_parts(up)
        act[b] = active.astype(BF16)
        pre_grad[b] = (cotangent * slope).astype(BF16)

    def some(h):
        return slice(2 * h, 2 * h + 2)

    def grad_sib(b, h):
        return copy(
            grads.at[1 - core, b, :, some(h)], grads_sib.at[b, :, some(h)], g_send.at[b, h], g_recv.at[b, h], to_sib
        )

    def weight_grads(b):
        for i in range(NC):
            c = feature(i)
            down = contract_first(act[b], tokens[1, c].reshape(m, width)).astype(BF16)
            grads[1, b, :, i] = down.reshape(ny, slab, width)
            upper = dot(tokens_t[c], pre_grad[b]).astype(BF16)
            for d in range(ny):
                for j in range(pieces):
                    base = (pieces * d + j) * slab
                    grads[0, b, d, i, :, j * w : (j + 1) * w] = upper[base : base + slab, :]
            if i % 2 == 1:
                grad_sib(b, i // 2).start()

    def y_copy(b, step, way, h):
        slot = wrap(depth, (1 if way == 0 else -1) * (ny // 2 - step), ny)
        these = some(h) if step > 0 else slice(2 * h + way, 2 * h + way + 1)
        return copy(
            grads.at[core, b, slot, these], grads_in.at[b, step, way, these],
            y_send.at[b, step, way, h], y_recv.at[b, step, way, h], to_y[way],
        )

    def back_copy(b, there):
        return copy(
            grads_own.at[b, there], grads_back.at[core, half_of, b],
            b_send.at[b, there], b_recv.at[core, half_of, b], peer(feature(there), holder),
        )

    def grads_y(b, step, h):
        if step == 0:
            got(grads_sib.at[b, :, some(h)], g_recv.at[b, h])
            grads[core, b, :, some(h)] = add(grads[core, b, :, some(h)], grads_sib[b, :, some(h)])
        if step < ny // 2:
            for way in range(2):
                slot = wrap(depth, (1 if way == 0 else -1) * (ny // 2 - step), ny)
                these = some(h) if step > 1 else slice(2 * h + way, 2 * h + way + 1)
                if step > 0:
                    y_copy(b, step - 1, way, h).wait_recv()
                    grads[core, b, slot, these] = add(grads[core, b, slot, these], grads_in[b, step - 1, way, these])
                y_copy(b, step, way, h).start()
            return
        for way in range(2):
            y_copy(b, step - 1, way, h).wait_recv()
        these = some(h)
        total = grads[core, b, depth, these].astype(F32) + grads_in[b, step - 1, 0, these].astype(F32) + grads_in[b, step - 1, 1, these].astype(F32)
        grads_own[b, these] = total.astype(BF16)
        for there in (2 * h, 2 * h + 1):
            if there < NC - 1:
                back_copy(b, there).start()
                continue

            @pl.when(core == holder)
            def _():
                grads_back[core, half_of, b] = grads_own[b, NC - 1]

            @pl.when(core != holder)
            def _():
                back_copy(b, NC - 1).start()

    targets = (x_far, x_right, x_left, x)

    def back_ref(e, step, way):
        slot = wrap(z, (1 if way == 0 else -1) * (NZ // 2 - step), NZ)
        return (targets[e], slot // 2, lax.rem(slot, 2), *((cut(way),) if step < 2 else ()))

    def back_z_copy(e, step, way):
        slot = back_ref(e, step, way)
        src, dst = slot[:3] if step else slot, (e, step, way, *((cut(way),) if step == 0 else ()))
        return copy(back.at[src], back_in.at[dst], v_send.at[e, step, way], v_recv.at[e, step, way], to_z[way])

    def back_x_copy(step, way):
        if step == 0:
            src, dst = back_own.at[0, cut(way)], back_half.at[way, cut(way)]
        else:
            src, dst = back_own.at[1 + way], back_full.at[way]
        return copy(src, dst, c_send.at[step, way], c_recv.at[step, way], to_x[way])

    def inputs():
        cotangent = jnp.concatenate([pre_grad[b] for b in range(parts)], axis=1)
        for i in range(NC):
            weight = jnp.concatenate([up_share[b, i] for b in range(parts)], axis=1)
            sums = contract_last(cotangent, weight).astype(BF16)
            back[:, feature(i)] = sums.reshape(NX, 2, block, width)
        for e in range(NX):
            for way in range(2):
                back_z_copy(e, 0, way).start()

    def back_z(e, step):
        for way in range(2):
            back_z_copy(e, step - 1, way).wait_recv()
            if step < NZ // 2:
                index = back_ref(e, step, way)
                landed = back_in[e, step - 1, way, cut(way)] if step == 1 else back_in[e, step - 1, way]
                back[index] = add(back[index], landed)
                back_z_copy(e, step, way).start()
        if step == NZ // 2:
            total = back[targets[e], k, zl].astype(F32) + back_in[e, step - 1, 0].astype(F32) + back_in[e, step - 1, 1].astype(F32)
            back_own[e] = total.astype(BF16)
            if e == 0:
                for way in range(2):
                    back_x_copy(0, way).start()

    def back_x(step):
        for way in range(2):
            back_x_copy(step, way).wait_recv()
            if step == 0:
                back_own[1 + way, cut(way)] = add(back_own[1 + way, cut(way)], back_half[way, cut(way)])
                back_x_copy(1, way).start()
        if step == 1:
            total = back_own[3].astype(F32) + back_full[0].astype(F32) + back_full[1].astype(F32)
            token_sums[1] = total.astype(BF16)

    order = tuple((dc, flip) for dc in (2, 1, 3, 0) for flip in (0, 1))

    def place(n):
        dc, flip = order[n]
        return wrap(k, dc, NC), (zl if flip == 0 else 1 - zl)

    def out_copy(n, step, way):
        c, zs = place(n)
        if step == 0:
            src, dst = out.at[x_far, c, zs, cut(way)], out_half.at[n, way]
        else:
            src, dst = out.at[x_right if way == 0 else x_left, c, zs], out_full.at[n, way]
        return copy(src, dst, x_send.at[n, step, way], x_recv.at[n, step, way], to_x[way])

    def outputs():
        active = jnp.concatenate([act[b] for b in range(parts)], axis=1)
        for i in range(NC):
            dc = order[2 * i][0]
            there = (dc - 1) % NC
            weight = jnp.concatenate([down_share(b, there) for b in range(parts)], axis=0)
            out[:, feature(there)] = dot(active, weight).astype(BF16).reshape(NX, 2, block, width)
            for n in (2 * i, 2 * i + 1):
                for way in range(2):
                    out_copy(n, 0, way).start()

    def out_x(n, step):
        c, zs = place(n)
        for way in range(2):
            out_copy(n, step - 1, way).wait_recv()
            if step == 1:
                to_ = x_right if way == 0 else x_left
                out[to_, c, zs, cut(way)] = add(out[to_, c, zs, cut(way)], out_half[n, way])
                out_copy(n, 1, way).start()
        if step == 2:
            total = out[x, c, zs].astype(F32) + out_full[n, 0].astype(F32) + out_full[n, 1].astype(F32)
            ring[2 * c + zs] = total.astype(BF16)

    def z_copy(step, way):
        slot = wrap(z, (1 if way == 0 else -1) * (NZ // 2 - step), NZ)
        src, dst = ring.at[slot], ring_in.at[step, way]
        if step == 0:
            src, dst = ring.at[slot, cut(way)], ring_in.at[0, way, cut(way)]
        return copy(src, dst, z_send.at[step, way], z_recv.at[step, way], to_z[way])

    def out_z(step):
        for way in range(2):
            slot = wrap(z, (1 if way == 0 else -1) * (NZ // 2 - step), NZ)
            if step > 0:
                z_copy(step - 1, way).wait_recv()
            if step == 1:
                ring[slot, cut(way)] = add(ring[slot, cut(way)], ring_in[0, way, cut(way)])
            elif 1 < step < NZ // 2:
                ring[slot] = add(ring[slot], ring_in[step - 1, way])
            if step < NZ // 2:
                z_copy(step, way).start()
        if step == NZ // 2:
            total = ring[z].astype(F32) + ring_in[step - 1, 0].astype(F32) + ring_in[step - 1, 1].astype(F32)
            token_sums[0] = total.astype(BF16)

    def drain_gathers():
        for way in range(2):
            for step in range(1, NZ // 2 + 1):
                for e in range(4):
                    ring_copy(2, streams[e], step, way, uz_send.at[e], uz_recv.at[e]).wait_send()
                for g in range(2):
                    tz_copy(g, step, way).wait_send()
            for step in range(2):
                for n in range(8):
                    for g in range(2):
                        tx_copy(g, n, step, way).wait_send()
                ux_copy(step, way).wait_send()
            for b in range(parts):
                for step in range(1, ny // 2 + 1):
                    w_copy(b, step, way).wait_send()
        for h in range(2):
            @pl.when(2 * core + h != k)
            def _():
                for array in range(2):
                    for b in range(parts):
                        pass_copy(array, b, h).wait_send()
        for b in range(parts):
            w_sib(b).wait_send()

        @pl.when(core == holder)
        def _():
            for one in own_copies():
                one.wait_send()

    def drain_sums():
        for way in range(2):
            for step in range(NZ // 2):
                for e in range(4):
                    back_z_copy(e, step, way).wait_send()
                z_copy(step, way).wait_send()
            for step in range(2):
                for n in range(8):
                    out_copy(n, step, way).wait_send()
                back_x_copy(step, way).wait_send()
            for b in range(parts):
                for step in range(ny // 2):
                    for h in range(2):
                        y_copy(b, step, way, h).wait_send()
        for b in range(parts):
            for h in range(2):
                grad_sib(b, h).wait_send()

    steps = dict(
        cx=cotangent_x, cz=cotangent_z, nz=normed_z, nx=normed_x, prep=prepare, own_out=own_out, own_in=own_in,
        wy=weights_y, w_in=weights_in, tok_in=tokens_in, F=forward, wg=weight_grads, gy=grads_y,
        inputs=inputs, outputs=outputs, bz=back_z, bx=back_x, ox=out_x, oz=out_z, drain=drain_gathers,
    )
    for name, *index in ORDER:
        steps[name](*index)

    drain_sums()

    for h in range(2):
        for array in range(2):
            local = jnp.logical_and(2 * core + h == k, core == array)

            @pl.when(jnp.logical_not(local))
            def _():
                for b in range(parts):
                    got(grads_back.at[array, h, b], b_recv.at[array, h, b])

    for h in range(2):
        for b in range(parts):
            base = (h * parts + b) * slab
            weight_sums[1, base : base + slab, :] = grads_back[1, h, b]
    columns = [
        jnp.concatenate([grads_back[0, h, b, :, i * w : (i + 1) * w] for i in range(pieces)], axis=0)
        for h in range(2) for b in range(parts)
    ]
    weight_sums[0] = contract_last(jnp.concatenate(columns, axis=1), perm[...]).astype(BF16)

    for b in range(parts):
        for there in range(NC - 1):
            back_copy(b, there).wait_send()

        @pl.when(core != holder)
        def _():
            back_copy(b, NC - 1).wait_send()


def finish(factor, token_sums, weight_sums, branch_out, normed_grad, up_grad, down_grad):
    branch_out[...] = token_sums[0]
    normed_grad[...] = token_sums[1]
    up_grad[...] = weight_sums[0].astype(F32) * factor
    down_grad[...] = weight_sums[1].astype(F32) * factor


def solution(mesh):
    n_row, n_depth = mesh.shape["row"], mesh.shape["depth"]

    def per_device(normed, up_weight, down_weight, out_grad):
        block, width = normed.shape
        hidden = up_weight.shape[1]
        m = block * n_row // 2
        parts = PARTS
        slab = hidden // 2 // parts // n_depth
        w = slab * n_depth
        factor = 1.0 / math.sqrt(block * n_row * n_depth)
        dma = pltpu.SemaphoreType.DMA
        vmem = pltpu.VMEM
        whole = pl.BlockSpec(memory_space=pltpu.VMEM)
        y_half = n_depth // 2
        token_sums, weight_sums = pl.pallas_call(
            functools.partial(kernel, (block, m, parts, slab, n_depth)),
            out_shape=(
                jax.ShapeDtypeStruct((2, block, width), BF16),
                jax.ShapeDtypeStruct((2, hidden // n_depth, width), BF16),
            ),
            in_specs=[whole, pl.BlockSpec(memory_space=pl.ANY), pl.BlockSpec(memory_space=pl.ANY), whole],
            out_specs=[whole] * 2,
            scratch_shapes=[
                vmem((width, hidden), BF16),
                vmem((hidden, width), BF16),
                dma((2,)),
                vmem((2, NC, NX, 2, block, width), BF16),
                vmem((NC, width, m), BF16),
                vmem((hidden, hidden), BF16),
                vmem((2, 2, parts, slab, width), BF16),
                vmem((2, parts, n_depth, NC, slab, width), BF16),
                vmem((parts, NC, width, w), BF16),
                vmem((parts, m, w), BF16),
                vmem((parts, m, w), BF16),
                vmem((2, parts, n_depth, NC, slab, width), BF16),
                vmem((parts, n_depth, NC, slab, width), BF16),
                vmem((parts, y_half, 2, NC, slab, width), BF16),
                vmem((parts, NC, slab, width), BF16),
                vmem((2, 2, parts, slab, width), BF16),
                vmem((NX, NC, 2, block, width), BF16),
                vmem((8, 2, block // 2, width), BF16),
                vmem((8, 2, block, width), BF16),
                vmem((NZ, block, width), BF16),
                vmem((NZ // 2, 2, block, width), BF16),
                vmem((NX, NC, 2, block, width), BF16),
                vmem((NX, NZ // 2, 2, block, width), BF16),
                vmem((NX, block, width), BF16),
                vmem((2, block, width), BF16),
                vmem((2, block, width), BF16),
                dma((2, NZ // 2, 2)), dma((2, NZ // 2, 2)),
                dma((2, 8, 2, 2)), dma((2, 8, 2, 2)),
                dma((2, 2)), dma((2, 2)),
                dma((NX, NZ // 2, 2)), dma((NX, NZ // 2, 2)),
                dma((2, 2, parts)), dma((parts, NC - 1)),
                dma((parts, y_half, 2)), dma((parts, y_half, 2)),
                dma((parts + 2,)), dma((parts + 2,)),
                dma((parts, 2)), dma((parts, 2)),
                dma((parts, y_half, 2, 2)), dma((parts, y_half, 2, 2)),
                dma((parts, NC)), dma((2, 2, parts)),
                dma((8, 2, 2)), dma((8, 2, 2)),
                dma((NZ // 2, 2)), dma((NZ // 2, 2)),
                dma((NX, NZ // 2, 2)), dma((NX, NZ // 2, 2)),
                dma((2, 2)), dma((2, 2)),
            ],
            compiler_params=pltpu.CompilerParams(
                collective_id=0, has_side_effects=True, vmem_limit_bytes=56 * 1024 * 1024
            ),
            cost_estimate=pl.CostEstimate(flops=4_000_000_000, bytes_accessed=4_000_000, transcendentals=400_000),
        )(normed, up_weight, down_weight, out_grad)
        return pl.pallas_call(
            functools.partial(finish, factor),
            out_shape=(
                jax.ShapeDtypeStruct((block, width), BF16),
                jax.ShapeDtypeStruct((block, width), BF16),
                jax.ShapeDtypeStruct((width // n_depth, hidden), F32),
                jax.ShapeDtypeStruct((hidden // n_depth, width), F32),
            ),
        )(token_sums, weight_sums)

    return jax.shard_map(
        per_device,
        mesh=mesh,
        in_specs=(P(("depth", "row"), "col"), P("col", "row"), P("row", "col"), P(("depth", "row"), "col")),
        out_specs=(
            P(("depth", "row"), "col"),
            P(("depth", "row"), "col"),
            P(("col", "depth"), "row"),
            P(("row", "depth"), "col"),
        ),
        check_vma=False,
    )
```

```python
import functools
import math

import jax
import jax.numpy as jnp
from jax import lax
from jax.experimental import pallas as pl
from jax.experimental.pallas import tpu as pltpu
from jax.sharding import PartitionSpec as P

MESH = pl.DeviceIdType.MESH
BF16, F32 = jnp.bfloat16, jnp.float32
NX, NZ, NC = 4, 8, 4
PARTS = 3
ORDER = (
    ("nz", 1), ("cx", 0), ("prep",), ("own_out",), ("nz", 2), ("nx", 0, 1), ("cx", 1), ("cz", 0, 2), ("own_in",),
    ("wy", 0, 1), ("nx", 1, 1), ("wy", 1, 1), ("nx", 2, 1), ("nx", 0, 2), ("cx", 2), ("wy", 2, 1), ("nx", 1, 2),
    ("wy", 0, 2), ("nz", 3), ("cz", 1, 2), ("nx", 2, 2), ("cz", 2, 2), ("wy", 1, 2), ("cz", 0, 3), ("cz", 3, 2),
    ("wy", 2, 2), ("nx", 3, 1), ("nz", 4), ("cz", 1, 3), ("wy", 0, 3), ("cz", 2, 3), ("nx", 4, 1), ("cz", 0, 4),
    ("wy", 1, 3), ("cz", 3, 3), ("nx", 3, 2), ("nz", 5), ("wy", 2, 3), ("cz", 1, 4), ("nx", 5, 1), ("cz", 2, 4),
    ("cz", 0, 5), ("wy", 0, 4), ("nx", 6, 1), ("cz", 3, 4), ("nx", 4, 2), ("wy", 1, 4), ("cz", 1, 5), ("cz", 2, 5),
    ("nx", 7, 1), ("wy", 2, 4), ("nx", 5, 2), ("wy", 0, 5), ("cz", 3, 5), ("nx", 6, 2), ("wy", 1, 5), ("w_in", 0),
    ("nx", 7, 2), ("tok_in",), ("wy", 2, 5), ("F", 0), ("wg", 0), ("w_in", 2), ("F", 2), ("wg", 2), ("gy", 0, 0, 1),
    ("gy", 0, 0, 0), ("w_in", 1), ("F", 1), ("wg", 1), ("gy", 2, 0, 0), ("inputs",), ("gy", 0, 1, 0), ("gy", 0, 1, 1),
    ("outputs",), ("gy", 1, 0, 0), ("gy", 1, 0, 1), ("gy", 2, 0, 1), ("gy", 2, 1, 0), ("bz", 0, 1), ("bz", 1, 1),
    ("gy", 0, 2, 0), ("drain",), ("bz", 2, 1), ("ox", 0, 1), ("bz", 3, 1), ("gy", 0, 2, 1), ("ox", 1, 1),
    ("gy", 1, 1, 0), ("ox", 2, 1), ("gy", 1, 1, 1), ("ox", 3, 1), ("gy", 2, 1, 1), ("ox", 4, 1), ("bz", 0, 2),
    ("ox", 5, 1), ("gy", 2, 2, 0), ("ox", 6, 1), ("bz", 1, 2), ("ox", 7, 1), ("gy", 0, 3, 0), ("bz", 2, 2),
    ("ox", 0, 2), ("oz", 0), ("gy", 0, 3, 1), ("bz", 3, 2), ("ox", 1, 2), ("gy", 1, 2, 0), ("bz", 0, 3), ("ox", 2, 2),
    ("gy", 1, 2, 1), ("bz", 1, 3), ("ox", 3, 2), ("gy", 2, 2, 1), ("bz", 2, 3), ("ox", 4, 2), ("gy", 2, 3, 0),
    ("ox", 5, 2), ("oz", 1), ("gy", 0, 4, 0), ("bz", 3, 3), ("ox", 6, 2), ("gy", 0, 4, 1), ("bz", 0, 4), ("ox", 7, 2),
    ("gy", 1, 3, 0), ("bz", 1, 4), ("gy", 1, 3, 1), ("bz", 2, 4), ("gy", 2, 3, 1), ("oz", 2), ("bx", 0),
    ("gy", 2, 4, 0), ("gy", 1, 4, 0), ("bz", 3, 4), ("gy", 1, 4, 1), ("gy", 2, 4, 1), ("bx", 1), ("oz", 3), ("oz", 4),
)
FIRST = 2


def dot(left, right):
    return jnp.dot(left, right, preferred_element_type=F32)


def contract_last(left, right):
    return lax.dot_general(left, right, (((1,), (1,)), ((), ())), preferred_element_type=F32)


def contract_first(left, right):
    return lax.dot_general(left, right, (((0,), (0,)), ((), ())), preferred_element_type=F32)


def gelu_parts(value):
    coeff = math.sqrt(2.0 / math.pi)
    square = value * value
    tangent = jnp.tanh(coeff * (value + 0.044715 * square * value))
    half = 0.5 * (1.0 + tangent)
    slope = half + 0.5 * value * (1.0 - tangent * tangent) * coeff * (1.0 + 3.0 * 0.044715 * square)
    return value * half, slope


def add(first, second):
    return (first.astype(F32) + second.astype(F32)).astype(BF16)


def wrap(index, by, size):
    return lax.rem(index + by + size, size)


def kernel(
    shape,
    normed_hbm, up_hbm, down_hbm, out_grad_hbm,
    token_sums, weight_sums,
    up_weight, down_weight, load,
    tokens, tokens_t, perm, w_own, weights, up_share,
    act, pre_grad, grads, grads_sib, grads_in, grads_own, grads_back,
    out, out_half, out_full, ring, ring_in, back, back_in, back_own, back_half, back_full,
    tz_send, tz_recv, tx_send, tx_recv, ux_send, ux_recv, uz_send, uz_recv,
    a_send, a_recv, w_send, w_recv, s_send, s_recv,
    g_send, g_recv, y_send, y_recv, b_send, b_recv,
    x_send, x_recv, z_send, z_recv, v_send, v_recv, c_send, c_recv,
):
    block, m, parts, slab, ny = shape
    width = normed_hbm.shape[1]
    hidden = up_weight.shape[1]
    w = slab * ny
    pieces = width // w
    share = parts * w
    lanes = width // 2
    first = FIRST * w
    row, k, depth = lax.axis_index("row"), lax.axis_index("col"), lax.axis_index("depth")
    x, zl, core = row // 4, lax.rem(row // 2, 2), lax.rem(row, 2)
    z = 2 * k + zl
    holder, half_of = k // 2, lax.rem(k, 2)

    def at(x_, z_, core_):
        return {"row": x_ * 4 + lax.rem(z_, 2) * 2 + core_, "col": z_ // 2}

    def peer(k_, core_):
        return {"row": x * 4 + zl * 2 + core_, "col": k_}

    x_right, x_left, x_far = wrap(x, 1, NX), wrap(x, -1, NX), wrap(x, 2, NX)
    to_x = (at(x_right, z, core), at(x_left, z, core))
    to_z = (at(x, wrap(z, 1, NZ), core), at(x, wrap(z, -1, NZ), core))
    to_y = ({"depth": wrap(depth, 1, ny)}, {"depth": wrap(depth, -1, ny)})
    to_sib = peer(k, 1 - core)

    def copy(src, dst, send, recv, to):
        return pltpu.make_async_remote_copy(
            src_ref=src, dst_ref=dst, send_sem=send, recv_sem=recv, device_id=to, device_id_type=MESH
        )

    def got(dst, recv):
        copy(dst, dst, recv, recv, to_sib).wait_recv()

    def sent(src, send):
        copy(src, src, send, send, to_sib).wait_send()

    def cut(way):
        return slice(way * (block // 2), (way + 1) * (block // 2))

    def lane_cut(way):
        return slice(way * lanes, (way + 1) * lanes)

    barrier = pltpu.get_barrier_semaphore()
    others = [peer(wrap(k, by, NC), core_) for by in (1, 2, 3) for core_ in (0, 1)]
    partners = (*to_x, *to_z, *to_y, to_sib, *others)
    for to in partners:
        pl.semaphore_signal(barrier, inc=1, device_id=to, device_id_type=MESH)
    own = (
        pltpu.make_async_copy(normed_hbm, tokens.at[0, k, x, zl], load.at[2]),
        pltpu.make_async_copy(out_grad_hbm, tokens.at[1, k, x, zl], load.at[3]),
    )
    loads = (pltpu.make_async_copy(up_hbm, up_weight, load.at[0]), pltpu.make_async_copy(down_hbm, down_weight, load.at[1]))
    for one in (*own, *loads):
        one.start()
    for one in own:
        one.wait()
    pl.semaphore_wait(barrier, len(partners))

    segments = ((0, slice(0, width)), (1, slice(0, first)), (1, slice(first, width)))

    def ref(segment, x_, slot, way=None):
        array, columns = segments[segment]
        return tokens.at[array, slot // 2, x_, lax.rem(slot, 2), slice(0, block) if way is None else cut(way), columns]

    def z_slot(step, way):
        return wrap(z, -(1 if way == 0 else -1) * step, NZ)

    def ring_copy(segment, x_, step, way, send, recv):
        view = ref(segment, x_, z_slot(step - 1, way), None if step < NZ // 2 else way)
        return copy(view, view, send.at[step - 1, way], recv.at[step - 1, way], to_z[way])

    def ring_got(segment, x_, step, way, recv):
        got(ref(segment, x_, z_slot(step, way), None if step < NZ // 2 else way), recv.at[step - 1, way])

    offsets = (0, -1, 1, -2, 2, -3, 3, 4)

    def tz_copy(g, step, way):
        return ring_copy(g, x, step, way, tz_send.at[g], tz_recv.at[g])

    def tx_copy(g, n, step, way):
        slot = wrap(z, offsets[n], NZ)
        view = ref(g, x, slot) if step == 0 else ref(g, x_left if way == 0 else x_right, slot, way)
        return copy(view, view, tx_send.at[g, n, step, way], tx_recv.at[g, n, step, way], to_x[way])

    def normed_z(step):
        for way in range(2):
            for g in range(2):
                if step > 1:
                    ring_got(g, x, step - 1, way, tz_recv.at[g])
                if step <= NZ // 2:
                    tz_copy(g, step, way).start()
            if 1 < step <= NZ // 2:
                for way_x in range(2):
                    for g in range(2):
                        tx_copy(g, 2 * (step - 1) - 1 + way, 0, way_x).start()
        if step == 1 or step == NZ // 2 + 1:
            for way_x in range(2):
                for g in range(2):
                    tx_copy(g, 0 if step == 1 else 7, 0, way_x).start()

    def normed_x(n, step):
        slot = wrap(z, offsets[n], NZ)
        for way in range(2):
            for g in range(2):
                if step == 1:
                    got(ref(g, x_left if way == 0 else x_right, slot), tx_recv.at[g, n, 0, way])
                    tx_copy(g, n, 1, way).start()
                else:
                    got(ref(g, x_far, slot, way), tx_recv.at[g, n, 1, way])

    def ux_copy(step, way):
        view = ref(2, x, z) if step == 0 else ref(2, x_left if way == 0 else x_right, z, way)
        return copy(view, view, ux_send.at[step, way], ux_recv.at[step, way], to_x[way])

    streams = (x, x_left, x_right, x_far)

    def cotangent_x(step):
        for way in range(2):
            if step == 1:
                got(ref(2, x_left if way == 0 else x_right, z), ux_recv.at[0, way])
                ux_copy(1, way).start()
            elif step == 2:
                got(ref(2, x_far, z, way), ux_recv.at[1, way])
            else:
                ux_copy(0, way).start()
        for e in ((0,), (1, 2), (3,))[step]:
            cotangent_z(e, 1)

    def cotangent_z(e, step):
        for way in range(2):
            if step > 1:
                ring_got(2, streams[e], step - 1, way, uz_recv.at[e])
            if step <= NZ // 2:
                ring_copy(2, streams[e], step, way, uz_send.at[e], uz_recv.at[e]).start()

    rows = hidden // ny

    def pass_on(b):
        for h in range(2):
            @pl.when(2 * core + h != k)
            def _():
                for array in range(2):
                    pass_copy(array, b, h).start()

    def pass_copy(array, b, h):
        to = 2 * core + h
        there = lax.rem(k - to + NC - 1, NC)
        return copy(
            w_own.at[h, array, b], weights.at[array, b, depth, there],
            a_send.at[h, array, b], a_recv.at[b, there], peer(to, array),
        )

    def prepare():
        for one in loads:
            one.wait()
        for h in range(2):
            for b in range(parts):
                w_own[h, 1, b] = down_weight[pl.ds(pl.multiple_of(depth * rows + (h * parts + b) * slab, slab), slab), :]
        inner = lax.broadcasted_iota(jnp.int32, (hidden, w), 1)
        index = (inner // slab) * rows + lax.rem(inner, slab)
        index = lax.broadcasted_iota(jnp.int32, (hidden, w), 0) - index
        mine = up_weight[pl.ds(pl.multiple_of(depth * rows, rows), rows), :]
        for b in range(parts):
            picks = [jnp.where(index == (h * parts + b) * slab, 1.0, 0.0).astype(BF16) for h in range(2)]
            mixed = dot(mine, jnp.concatenate(picks, axis=1)).astype(BF16)
            for h in range(2):
                g = h * parts + b
                perm[:, g * w : (g + 1) * w] = picks[h]
                for i in range(pieces):
                    w_own[h, 0, b, :, i * w : (i + 1) * w] = mixed[i * slab : (i + 1) * slab, h * w : (h + 1) * w]
            pass_on(b)

    def own_copies():
        return (
            copy(weights.at[1, :, :, NC - 1], weights.at[1, :, :, NC - 1], s_send.at[parts], s_recv.at[parts], to_sib),
            copy(up_share.at[:, NC - 1], up_share.at[:, NC - 1], s_send.at[parts + 1], s_recv.at[parts + 1], to_sib),
        )

    def own_out():
        @pl.when(core == holder)
        def _():
            for b in range(parts):
                for d in range(ny):
                    base = d * rows + half_of * (parts * slab) + b * slab
                    weights[1, b, d, NC - 1] = down_weight[pl.ds(pl.multiple_of(base, slab), slab), :]
            here = pl.ds(pl.multiple_of(half_of * share, share), share)
            up_own = dot(up_weight[...], perm[:, here]).astype(BF16)
            for b in range(parts):
                up_share[b, NC - 1] = up_own[:, b * w : (b + 1) * w]
            for one in own_copies():
                one.start()

    def own_in():
        @pl.when(core != holder)
        def _():
            got(weights.at[1, :, :, NC - 1], s_recv.at[parts])
            got(up_share.at[:, NC - 1], s_recv.at[parts + 1])

    def w_ref(b, step, way):
        slot = wrap(depth, -(1 if way == 0 else -1) * step, ny)
        if step < ny // 2:
            return weights.at[core, b, slot, 0 : NC - 1]
        return weights.at[core, b, slot, 0 : NC - 1, :, lane_cut(way)]

    def w_copy(b, step, way):
        slot = wrap(depth, -(1 if way == 0 else -1) * (step - 1), ny)
        view = weights.at[core, b, slot, 0 : NC - 1]
        if step == ny // 2:
            view = weights.at[core, b, slot, 0 : NC - 1, :, lane_cut(way)]
        return copy(view, view, w_send.at[b, step - 1, way], w_recv.at[b, step - 1, way], to_y[way])

    def w_sib(b):
        view = weights.at[core, b, :, 0 : NC - 1]
        return copy(view, view, s_send.at[b], s_recv.at[b], to_sib)

    def weights_y(b, step):
        if step == 1:
            for there in range(NC - 1):
                got(weights.at[core, b, depth, there], a_recv.at[b, there])
        for way in range(2):
            if step > 1:
                got(w_ref(b, step - 1, way), w_recv.at[b, step - 2, way])
            if step <= ny // 2:
                w_copy(b, step, way).start()
        if step == ny // 2 + 1:
            w_sib(b).start()

    def weights_in(b):
        got(weights.at[1 - core, b, :, 0 : NC - 1], s_recv.at[b])
        for there in range(NC - 1):
            for d in range(ny):
                for i in range(pieces):
                    base = (pieces * d + i) * slab
                    up_share[b, there, base : base + slab, :] = weights[0, b, d, there, :, i * w : (i + 1) * w]

    def feature(there):
        return wrap(k, 1 + there, NC)

    def tokens_in():
        for c in range(NC):
            tokens_t[c] = tokens[0, c].reshape(m, width).T

    def down_share(b, there):
        return weights[1, b, :, there].reshape(w, width)

    def forward(b):
        up = sum(dot(tokens[0, feature(i)].reshape(m, width), up_share[b, i]) for i in range(NC))
        cotangent = sum(contract_last(tokens[1, feature(i)].reshape(m, width), down_share(b, i)) for i in range(NC))
        active, slope = gelu_parts(up)
        act[b] = active.astype(BF16)
        pre_grad[b] = (cotangent * slope).astype(BF16)

    def some(h):
        return slice(2 * h, 2 * h + 2)

    def grad_sib(b, h):
        return copy(
            grads.at[1 - core, b, :, some(h)], grads_sib.at[b, :, some(h)], g_send.at[b, h], g_recv.at[b, h], to_sib
        )

    def weight_grads(b):
        for i in range(NC):
            c = feature(i)
            down = contract_first(act[b], tokens[1, c].reshape(m, width)).astype(BF16)
            grads[1, b, :, i] = down.reshape(ny, slab, width)
            upper = dot(tokens_t[c], pre_grad[b]).astype(BF16)
            for d in range(ny):
                for j in range(pieces):
                    base = (pieces * d + j) * slab
                    grads[0, b, d, i, :, j * w : (j + 1) * w] = upper[base : base + slab, :]
            if i % 2 == 1:
                grad_sib(b, i // 2).start()

    def y_copy(b, step, way, h):
        slot = wrap(depth, (1 if way == 0 else -1) * (ny // 2 - step), ny)
        these = some(h) if step > 0 else slice(2 * h + way, 2 * h + way + 1)
        return copy(
            grads.at[core, b, slot, these], grads_in.at[b, step, way, these],
            y_send.at[b, step, way, h], y_recv.at[b, step, way, h], to_y[way],
        )

    def back_copy(b, there):
        return copy(
            grads_own.at[b, there], grads_back.at[core, half_of, b],
            b_send.at[b, there], b_recv.at[core, half_of, b], peer(feature(there), holder),
        )

    def grads_y(b, step, h):
        if step == 0:
            got(grads_sib.at[b, :, some(h)], g_recv.at[b, h])
            grads[core, b, :, some(h)] = add(grads[core, b, :, some(h)], grads_sib[b, :, some(h)])
        if step < ny // 2:
            for way in range(2):
                slot = wrap(depth, (1 if way == 0 else -1) * (ny // 2 - step), ny)
                these = some(h) if step > 1 else slice(2 * h + way, 2 * h + way + 1)
                if step > 0:
                    y_copy(b, step - 1, way, h).wait_recv()
                    grads[core, b, slot, these] = add(grads[core, b, slot, these], grads_in[b, step - 1, way, these])
                y_copy(b, step, way, h).start()
            return
        for way in range(2):
            y_copy(b, step - 1, way, h).wait_recv()
        these = some(h)
        total = grads[core, b, depth, these].astype(F32) + grads_in[b, step - 1, 0, these].astype(F32) + grads_in[b, step - 1, 1, these].astype(F32)
        grads_own[b, these] = total.astype(BF16)
        for there in (2 * h, 2 * h + 1):
            if there < NC - 1:
                back_copy(b, there).start()
                continue

            @pl.when(core == holder)
            def _():
                grads_back[core, half_of, b] = grads_own[b, NC - 1]

            @pl.when(core != holder)
            def _():
                back_copy(b, NC - 1).start()

    targets = (x_far, x_right, x_left, x)

    def back_ref(e, step, way):
        slot = wrap(z, (1 if way == 0 else -1) * (NZ // 2 - step), NZ)
        return (targets[e], slot // 2, lax.rem(slot, 2), *((cut(way),) if step < 2 else ()))

    def back_z_copy(e, step, way):
        slot = back_ref(e, step, way)
        src, dst = slot[:3] if step else slot, (e, step, way, *((cut(way),) if step == 0 else ()))
        return copy(back.at[src], back_in.at[dst], v_send.at[e, step, way], v_recv.at[e, step, way], to_z[way])

    def back_x_copy(step, way):
        if step == 0:
            src, dst = back_own.at[0, cut(way)], back_half.at[way, cut(way)]
        else:
            src, dst = back_own.at[1 + way], back_full.at[way]
        return copy(src, dst, c_send.at[step, way], c_recv.at[step, way], to_x[way])

    def inputs():
        cotangent = jnp.concatenate([pre_grad[b] for b in range(parts)], axis=1)
        for i in range(NC):
            weight = jnp.concatenate([up_share[b, i] for b in range(parts)], axis=1)
            sums = contract_last(cotangent, weight).astype(BF16)
            back[:, feature(i)] = sums.reshape(NX, 2, block, width)
        for e in range(NX):
            for way in range(2):
                back_z_copy(e, 0, way).start()

    def back_z(e, step):
        for way in range(2):
            back_z_copy(e, step - 1, way).wait_recv()
            if step < NZ // 2:
                index = back_ref(e, step, way)
                landed = back_in[e, step - 1, way, cut(way)] if step == 1 else back_in[e, step - 1, way]
                back[index] = add(back[index], landed)
                back_z_copy(e, step, way).start()
        if step == NZ // 2:
            total = back[targets[e], k, zl].astype(F32) + back_in[e, step - 1, 0].astype(F32) + back_in[e, step - 1, 1].astype(F32)
            back_own[e] = total.astype(BF16)
            if e == 0:
                for way in range(2):
                    back_x_copy(0, way).start()

    def back_x(step):
        for way in range(2):
            back_x_copy(step, way).wait_recv()
            if step == 0:
                back_own[1 + way, cut(way)] = add(back_own[1 + way, cut(way)], back_half[way, cut(way)])
                back_x_copy(1, way).start()
        if step == 1:
            total = back_own[3].astype(F32) + back_full[0].astype(F32) + back_full[1].astype(F32)
            token_sums[1] = total.astype(BF16)

    order = tuple((dc, flip) for dc in (2, 1, 3, 0) for flip in (0, 1))

    def place(n):
        dc, flip = order[n]
        return wrap(k, dc, NC), (zl if flip == 0 else 1 - zl)

    def out_copy(n, step, way):
        c, zs = place(n)
        if step == 0:
            src, dst = out.at[x_far, c, zs, cut(way)], out_half.at[n, way]
        else:
            src, dst = out.at[x_right if way == 0 else x_left, c, zs], out_full.at[n, way]
        return copy(src, dst, x_send.at[n, step, way], x_recv.at[n, step, way], to_x[way])

    def outputs():
        active = jnp.concatenate([act[b] for b in range(parts)], axis=1)
        for i in range(NC):
            dc = order[2 * i][0]
            there = (dc - 1) % NC
            weight = jnp.concatenate([down_share(b, there) for b in range(parts)], axis=0)
            out[:, feature(there)] = dot(active, weight).astype(BF16).reshape(NX, 2, block, width)
            for n in (2 * i, 2 * i + 1):
                for way in range(2):
                    out_copy(n, 0, way).start()

    def out_x(n, step):
        c, zs = place(n)
        for way in range(2):
            out_copy(n, step - 1, way).wait_recv()
            if step == 1:
                to_ = x_right if way == 0 else x_left
                out[to_, c, zs, cut(way)] = add(out[to_, c, zs, cut(way)], out_half[n, way])
                out_copy(n, 1, way).start()
        if step == 2:
            total = out[x, c, zs].astype(F32) + out_full[n, 0].astype(F32) + out_full[n, 1].astype(F32)
            ring[2 * c + zs] = total.astype(BF16)

    def z_copy(step, way):
        slot = wrap(z, (1 if way == 0 else -1) * (NZ // 2 - step), NZ)
        src, dst = ring.at[slot], ring_in.at[step, way]
        if step == 0:
            src, dst = ring.at[slot, cut(way)], ring_in.at[0, way, cut(way)]
        return copy(src, dst, z_send.at[step, way], z_recv.at[step, way], to_z[way])

    def out_z(step):
        for way in range(2):
            slot = wrap(z, (1 if way == 0 else -1) * (NZ // 2 - step), NZ)
            if step > 0:
                z_copy(step - 1, way).wait_recv()
            if step == 1:
                ring[slot, cut(way)] = add(ring[slot, cut(way)], ring_in[0, way, cut(way)])
            elif 1 < step < NZ // 2:
                ring[slot] = add(ring[slot], ring_in[step - 1, way])
            if step < NZ // 2:
                z_copy(step, way).start()
        if step == NZ // 2:
            total = ring[z].astype(F32) + ring_in[step - 1, 0].astype(F32) + ring_in[step - 1, 1].astype(F32)
            token_sums[0] = total.astype(BF16)

    def drain_gathers():
        for way in range(2):
            for step in range(1, NZ // 2 + 1):
                for e in range(4):
                    ring_copy(2, streams[e], step, way, uz_send.at[e], uz_recv.at[e]).wait_send()
                for g in range(2):
                    tz_copy(g, step, way).wait_send()
            for step in range(2):
                for n in range(8):
                    for g in range(2):
                        tx_copy(g, n, step, way).wait_send()
                ux_copy(step, way).wait_send()
            for b in range(parts):
                for step in range(1, ny // 2 + 1):
                    w_copy(b, step, way).wait_send()
        for h in range(2):
            @pl.when(2 * core + h != k)
            def _():
                for array in range(2):
                    for b in range(parts):
                        pass_copy(array, b, h).wait_send()
        for b in range(parts):
            w_sib(b).wait_send()

        @pl.when(core == holder)
        def _():
            for one in own_copies():
                one.wait_send()

    def drain_sums():
        for way in range(2):
            for step in range(NZ // 2):
                for e in range(4):
                    back_z_copy(e, step, way).wait_send()
                z_copy(step, way).wait_send()
            for step in range(2):
                for n in range(8):
                    out_copy(n, step, way).wait_send()
                back_x_copy(step, way).wait_send()
            for b in range(parts):
                for step in range(ny // 2):
                    for h in range(2):
                        y_copy(b, step, way, h).wait_send()
        for b in range(parts):
            for h in range(2):
                grad_sib(b, h).wait_send()

    steps = dict(
        cx=cotangent_x, cz=cotangent_z, nz=normed_z, nx=normed_x, prep=prepare, own_out=own_out, own_in=own_in,
        wy=weights_y, w_in=weights_in, tok_in=tokens_in, F=forward, wg=weight_grads, gy=grads_y,
        inputs=inputs, outputs=outputs, bz=back_z, bx=back_x, ox=out_x, oz=out_z, drain=drain_gathers,
    )
    for name, *index in ORDER:
        steps[name](*index)

    drain_sums()

    for h in range(2):
        for array in range(2):
            local = jnp.logical_and(2 * core + h == k, core == array)

            @pl.when(jnp.logical_not(local))
            def _():
                for b in range(parts):
                    got(grads_back.at[array, h, b], b_recv.at[array, h, b])

    for h in range(2):
        for b in range(parts):
            base = (h * parts + b) * slab
            weight_sums[1, base : base + slab, :] = grads_back[1, h, b]
    columns = [
        jnp.concatenate([grads_back[0, h, b, :, i * w : (i + 1) * w] for i in range(pieces)], axis=0)
        for h in range(2) for b in range(parts)
    ]
    weight_sums[0] = contract_last(jnp.concatenate(columns, axis=1), perm[...]).astype(BF16)

    for b in range(parts):
        for there in range(NC - 1):
            back_copy(b, there).wait_send()

        @pl.when(core != holder)
        def _():
            back_copy(b, NC - 1).wait_send()


def finish(factor, token_any, weight_any, branch_out, normed_grad, up_grad, down_grad, token_sums, weight_sums, load):
    loads = (
        pltpu.make_async_copy(token_any, token_sums, load.at[0]),
        pltpu.make_async_copy(weight_any, weight_sums, load.at[1]),
    )
    for one in loads:
        one.start()
    for one in loads:
        one.wait()
    branch_out[...] = token_sums[0]
    normed_grad[...] = token_sums[1]
    up_grad[...] = weight_sums[0].astype(F32) * factor
    down_grad[...] = weight_sums[1].astype(F32) * factor


def solution(mesh):
    n_row, n_depth = mesh.shape["row"], mesh.shape["depth"]

    def per_device(normed, up_weight, down_weight, out_grad):
        block, width = normed.shape
        hidden = up_weight.shape[1]
        m = block * n_row // 2
        parts = PARTS
        slab = hidden // 2 // parts // n_depth
        w = slab * n_depth
        factor = 1.0 / math.sqrt(block * n_row * n_depth)
        dma = pltpu.SemaphoreType.DMA
        vmem = pltpu.VMEM
        whole = pl.BlockSpec(memory_space=pltpu.VMEM)
        y_half = n_depth // 2
        token_sums, weight_sums = pl.pallas_call(
            functools.partial(kernel, (block, m, parts, slab, n_depth)),
            out_shape=(
                pltpu.VMEM((2, block, width), BF16),
                pltpu.VMEM((2, hidden // n_depth, width), BF16),
            ),
            in_specs=[pl.BlockSpec(memory_space=pl.ANY)] * 4,
            out_specs=[whole] * 2,
            scratch_shapes=[
                vmem((width, hidden), BF16),
                vmem((hidden, width), BF16),
                dma((4,)),
                vmem((2, NC, NX, 2, block, width), BF16),
                vmem((NC, width, m), BF16),
                vmem((hidden, hidden), BF16),
                vmem((2, 2, parts, slab, width), BF16),
                vmem((2, parts, n_depth, NC, slab, width), BF16),
                vmem((parts, NC, width, w), BF16),
                vmem((parts, m, w), BF16),
                vmem((parts, m, w), BF16),
                vmem((2, parts, n_depth, NC, slab, width), BF16),
                vmem((parts, n_depth, NC, slab, width), BF16),
                vmem((parts, y_half, 2, NC, slab, width), BF16),
                vmem((parts, NC, slab, width), BF16),
                vmem((2, 2, parts, slab, width), BF16),
                vmem((NX, NC, 2, block, width), BF16),
                vmem((8, 2, block // 2, width), BF16),
                vmem((8, 2, block, width), BF16),
                vmem((NZ, block, width), BF16),
                vmem((NZ // 2, 2, block, width), BF16),
                vmem((NX, NC, 2, block, width), BF16),
                vmem((NX, NZ // 2, 2, block, width), BF16),
                vmem((NX, block, width), BF16),
                vmem((2, block, width), BF16),
                vmem((2, block, width), BF16),
                dma((2, NZ // 2, 2)), dma((2, NZ // 2, 2)),
                dma((2, 8, 2, 2)), dma((2, 8, 2, 2)),
                dma((2, 2)), dma((2, 2)),
                dma((NX, NZ // 2, 2)), dma((NX, NZ // 2, 2)),
                dma((2, 2, parts)), dma((parts, NC - 1)),
                dma((parts, y_half, 2)), dma((parts, y_half, 2)),
                dma((parts + 2,)), dma((parts + 2,)),
                dma((parts, 2)), dma((parts, 2)),
                dma((parts, y_half, 2, 2)), dma((parts, y_half, 2, 2)),
                dma((parts, NC)), dma((2, 2, parts)),
                dma((8, 2, 2)), dma((8, 2, 2)),
                dma((NZ // 2, 2)), dma((NZ // 2, 2)),
                dma((NX, NZ // 2, 2)), dma((NX, NZ // 2, 2)),
                dma((2, 2)), dma((2, 2)),
            ],
            compiler_params=pltpu.CompilerParams(
                collective_id=0, has_side_effects=True, vmem_limit_bytes=56 * 1024 * 1024
            ),
            cost_estimate=pl.CostEstimate(flops=4_000_000_000, bytes_accessed=4_000_000, transcendentals=400_000),
        )(normed, up_weight, down_weight, out_grad)
        return pl.pallas_call(
            functools.partial(finish, factor),
            out_shape=(
                jax.ShapeDtypeStruct((block, width), BF16),
                jax.ShapeDtypeStruct((block, width), BF16),
                jax.ShapeDtypeStruct((width // n_depth, hidden), F32),
                jax.ShapeDtypeStruct((hidden // n_depth, width), F32),
            ),
            in_specs=[pl.BlockSpec(memory_space=pl.ANY)] * 2,
            scratch_shapes=[
                vmem((2, block, width), BF16),
                vmem((2, hidden // n_depth, width), BF16),
                dma((2,)),
            ],
        )(token_sums, weight_sums)

    return jax.shard_map(
        per_device,
        mesh=mesh,
        in_specs=(P(("depth", "row"), "col"), P("col", "row"), P("row", "col"), P(("depth", "row"), "col")),
        out_specs=(
            P(("depth", "row"), "col"),
            P(("depth", "row"), "col"),
            P(("col", "depth"), "row"),
            P(("row", "depth"), "col"),
        ),
        check_vma=False,
    )
```
